32 devices in a mesh: groups: 2 (over x), dp: 8 (over z, y), owner: 2 (over core).
Axes of the slice: x: 2, y: 2, z: 4, core: 2. Of those that a mesh axis runs over, the one named last changes fastest.
Arguments:
- embeddings: float32 [32768, 1024], P(('groups', 'dp', 'owner')), parts along dimension 0, may hold values from -14 to 14
- cluster_ids: int32 [32768], P(('groups', 'dp', 'owner')), parts along dimension 0, may hold values from 0 to 63, as said below
Outputs:
- nearest: float32 [32768], P(('groups', 'dp', 'owner')), parts along dimension 0
The draws below stay inside these ranges and needn't reach their ends.
There are 2 independent parts, one for each index of `groups`. The reference program is written for one: setup_inputs(seed, part) draws one part's arguments, and reference() takes and returns one part's arrays. A program takes and returns all parts, laid end to end along the dimension named above; each array names one. Nothing has to cross between parts.
Inputs may be any that keep to these rules, and one draw needn't show every extreme that they name: `cluster_ids`: cluster c belongs to index c // 8 of dp. The examples of one device include at most 256 of the clusters of any one index of dp; in every draw one index of dp has exactly 256 from every device. Some clusters may have a single member.
All inputs are finite; a program needn't handle non-finite values.
Results may differ from the reference program's by a relative error of at most 0.00032.
Values may be sent and summed in bfloat16 or wider, within the bound.
No kernel may reach another device: no remote copies, remote signals or barrier semaphores. Data moves between devices by JAX's collectives and lax.ppermute only.
A program may use at most 64 MiB of HBM per device.

```python
import jax
import jax.numpy as jnp
from jax import lax

E = 1024
ROW_DEV = 1024
CL_DEV = 8
CAP = 256
ROWS = 16384
N_DP = 8
N_OWNER = 2


def member_ids(key):
    leader = jax.random.randint(jax.random.fold_in(key, 11), (), 0, N_DP)
    senders = N_DP * N_OWNER
    row_index = jnp.arange(ROW_DEV, dtype=jnp.int32)
    spread = (leader + 1 + (row_index - CAP) % (N_DP - 1)) % N_DP
    target = jnp.where(row_index < CAP, leader, spread).astype(jnp.int32)
    streams = jax.random.split(jax.random.fold_in(key, 12), senders)
    shuffled = jax.vmap(lambda single: jax.random.permutation(single, target))(streams)
    pick_one = jax.random.randint(jax.random.fold_in(key, 13), (senders, ROW_DEV), 0, CL_DEV - 1)
    pick_two = jax.random.randint(jax.random.fold_in(key, 14), (senders, ROW_DEV), 0, CL_DEV - 1)
    sender_index = jnp.arange(senders, dtype=jnp.int32)
    hits = (shuffled == sender_index[:, None]).astype(jnp.int32)
    first_hit = jnp.argmax(hits, axis=1).astype(jnp.int32)
    lonely = (row_index[None, :] == first_hit[:, None]) & (sender_index[:, None] < N_DP)
    picked = jnp.where(lonely, CL_DEV - 1, jnp.minimum(pick_one, pick_two))
    order = jnp.argsort(shuffled, axis=1, stable=True).astype(jnp.int32)
    first = order[:, :-1]
    second = order[:, 1:]
    first_target = jnp.take_along_axis(shuffled, first, axis=1)
    second_target = jnp.take_along_axis(shuffled, second, axis=1)
    first_lonely = jnp.take_along_axis(lonely, first, axis=1)
    second_lonely = jnp.take_along_axis(lonely, second, axis=1)
    step_index = jnp.arange(ROW_DEV - 1, dtype=jnp.int32)
    chosen = (step_index % 64 == 5)[None, :] & (first_target == second_target)
    chosen = chosen & jnp.logical_not(first_lonely) & jnp.logical_not(second_lonely)
    chosen_int = chosen.astype(jnp.int32)
    rows_at = jnp.broadcast_to(sender_index[:, None], first.shape)
    in_pair = jnp.zeros((senders, ROW_DEV), jnp.int32).at[rows_at, first].max(chosen_int)
    in_pair = in_pair.at[rows_at, second].max(chosen_int)
    source_pos = jnp.broadcast_to(row_index[None, :], (senders, ROW_DEV))
    source_pos = source_pos.at[rows_at, second].set(jnp.where(chosen, first, second))
    picked = jnp.where(in_pair > 0, 0, picked)
    labels = (shuffled * CL_DEV + picked).reshape(ROWS).astype(jnp.int32)
    source = (sender_index[:, None] * ROW_DEV + source_pos).reshape(ROWS).astype(jnp.int32)
    return (labels, source, in_pair.reshape(ROWS))


def draw_cluster_ids(key, part):
    labels, source, in_pair = member_ids(key)
    return labels


def draw_embeddings(key, part):
    labels, source, in_pair = member_ids(key)
    key = jax.random.fold_in(key, 5)
    centers = jax.random.truncated_normal(jax.random.fold_in(key, 1), -4.0, 4.0, (CL_DEV * N_DP, E), jnp.float32)
    weight_row = jax.random.uniform(jax.random.fold_in(key, 2), (ROWS, 1), jnp.float32, 0.2, 1.5)
    weight_row = jnp.where(in_pair[:, None] > 0, jnp.float32(0.2), weight_row)
    base = centers[labels] * weight_row
    noise = jax.random.truncated_normal(jax.random.fold_in(key, 4), -4.0, 4.0, (ROWS, E), jnp.float32)
    full = base + noise
    jitter = jax.random.truncated_normal(jax.random.fold_in(key, 7), -4.0, 4.0, (ROWS, E), jnp.float32)
    near = full[source] + 0.05 * jitter
    copies = (source != jnp.arange(ROWS, dtype=jnp.int32))[:, None]
    return jnp.where(copies, near, full)


def setup_inputs(seed: int = 0, part: int = 0) -> dict:
    seeds = jax.random.split(jax.random.key(seed), 3)
    part_keys = jax.random.split(jax.random.fold_in(seeds[2], part), 3)
    embeddings = draw_embeddings(jax.random.fold_in(jax.random.fold_in(seeds[2], part), 71), part)
    cluster_ids = draw_cluster_ids(jax.random.fold_in(jax.random.fold_in(seeds[2], part), 71), part)
    return {"embeddings": embeddings, "cluster_ids": cluster_ids}


def reference(embeddings, cluster_ids):
    squares = lax.optimization_barrier(jnp.sum(embeddings * embeddings, axis=1, keepdims=True))
    unit = (embeddings * lax.rsqrt(squares + 1e-06)).astype(jnp.bfloat16)
    target = (cluster_ids // CL_DEV).astype(jnp.int32)
    most = N_DP * N_OWNER * CAP

    def per_owner(index):
        order = jnp.argsort((target != index).astype(jnp.int32), stable=True)[:most].astype(jnp.int32)
        members = unit[order].astype(jnp.float32)
        labels = cluster_ids[order]
        live = target[order] == index
        scores = jnp.dot(members, members.T, precision=lax.Precision.HIGHEST, preferred_element_type=jnp.float32)
        same = (labels[:, None] == labels[None, :]) & live[None, :]
        same = same & ~jnp.eye(most, dtype=bool)
        best = lax.optimization_barrier(jnp.max(jnp.where(same, scores, jnp.float32(-1.0)), axis=1))
        return (jnp.where(live, best, jnp.float32(0.0)), order)
    values, orders = lax.map(per_owner, jnp.arange(N_DP, dtype=jnp.int32))
    nearest = jnp.zeros((ROWS,), jnp.float32).at[orders.reshape(-1)].add(values.reshape(-1))
    return nearest
```

```python
import functools
import math

import jax
import jax.numpy as jnp
from jax import lax
from jax.experimental import pallas as pl
from jax.experimental.pallas import tpu as pltpu
from jax.sharding import PartitionSpec as P

CL_DEV = 8
LANES = 128
SUB = 16
VMEM_LIMIT = 48 * 1024 * 1024
ANY = pl.BlockSpec(memory_space=pl.ANY)
VMEM = pl.BlockSpec(memory_space=pltpu.VMEM)
SMEM = pl.BlockSpec(memory_space=pltpu.SMEM)
NT = (((1,), (1,)), ((), ()))


def pad_lanes(row, width):
    extra = width - row.shape[1]
    if extra == 0:
        return row
    return jnp.concatenate([row, jnp.zeros((row.shape[0], extra), row.dtype)], axis=1)


def as_column(row):
    return jnp.transpose(jnp.broadcast_to(row, (8, row.shape[1])))[:, 0:1]


def code_of(leader, bad):
    return 16 + 2 * leader + bad


def lead_kernel(peers, cap, block, me_ref, ids_ref, emb_ref, unit_ref, info_ref, hdr_ref, lead_ref):
    count, width = emb_ref.shape
    ids = ids_ref[...]
    target = jnp.right_shift(ids, int(math.log2(CL_DEV)))
    local_id = jnp.bitwise_and(ids, CL_DEV - 1)
    tio = lax.broadcasted_iota(jnp.int32, (peers, 1), 0)
    onehot = (lax.broadcasted_iota(jnp.int32, (peers, count), 0) == target).astype(jnp.int32)
    lane = lax.broadcasted_iota(jnp.int32, (peers, count), 1)
    cum = onehot
    step = 1
    while step < count:
        cum = cum + jnp.where(lane >= step, pltpu.roll(cum, step, 1), 0)
        step *= 2
    rank = jnp.sum(cum * onehot, axis=0, keepdims=True) - 1
    counts = cum[:, count - 1 : count]
    leader = jnp.min(jnp.where(counts == cap, tio, peers - 1), axis=0, keepdims=True)
    others = jnp.max(jnp.where(tio == leader, cap - counts, counts), axis=0, keepdims=True)
    lead_short = jnp.max(jnp.where(tio == leader, cap - counts, 0), axis=0, keepdims=True)
    bad = ((others > block - 1) | (lead_short != 0)).astype(jnp.int32)
    is_lead = target == leader
    rel = target - me_ref[0]
    rel = jnp.where(rel < 0, rel + peers, rel)
    slots = peers * block
    fits = rank < block - 1
    dest = jnp.where(is_lead, slots + rank, jnp.where(fits, rel * block + rank, -1))
    pitch = -(-block // LANES) * LANES
    final = jnp.where(is_lead, peers * pitch + rank, target * pitch + rank)
    row8 = lax.broadcasted_iota(jnp.int32, (8, count), 0)
    info_ref[...] = jnp.where(row8 == 0, dest, final)

    both = jnp.where(row8 == 0, dest, local_id + 1).astype(jnp.float32)
    both = jnp.transpose(both)
    dest_col, id_col = both[:, 0:1], both[:, 1:2]
    pieces = []
    for start in range(0, slots + cap, LANES):
        at = (lax.broadcasted_iota(jnp.int32, (count, LANES), 1) + start).astype(jnp.float32)
        pieces.append(jnp.sum(jnp.where(dest_col == at, id_col, 0.0), axis=0, keepdims=True))
    ids_at = jnp.concatenate(pieces, axis=1)
    block_ids = ids_at[:, :slots]
    slot_lane = lax.broadcasted_iota(jnp.int32, (1, slots), 1)
    last = functools.reduce(jnp.logical_or, [slot_lane == k * block + block - 1 for k in range(peers)])
    code = code_of(leader, bad).astype(jnp.float32)
    block_ids = jnp.where(last, code, block_ids)
    hdr_ref[...] = jnp.broadcast_to(pad_lanes(block_ids, width), (8, width))

    emb = emb_ref[...]
    squares = jnp.sum(emb * emb, axis=1, keepdims=True)
    unit = (emb * lax.rsqrt(squares + 1e-06)).astype(jnp.bfloat16)
    unit_ref[...] = unit
    at = lax.broadcasted_iota(jnp.int32, (cap, count), 0) + slots
    pick = jnp.where(at == dest, 1.0, 0.0).astype(jnp.bfloat16)
    lead_ref[:cap, :] = jnp.dot(pick, unit, preferred_element_type=jnp.float32).astype(jnp.bfloat16)
    lead_hdr = pad_lanes(ids_at[:, slots:], width)
    lead_ref[cap:, :] = jnp.broadcast_to(lead_hdr, (SUB, width)).astype(jnp.bfloat16)


def pack_kernel(peers, block, unit_ref, info_ref, hdr_ref, *rest):
    outs, pick = rest[:peers], rest[peers]
    count, width = unit_ref.shape
    dest = info_ref[0:1, :]
    at = lax.broadcasted_iota(jnp.int32, (peers * block, count), 0)
    pick[...] = jnp.where(at == dest, 1.0, 0.0).astype(jnp.bfloat16)
    is_hdr = lax.broadcasted_iota(jnp.int32, (block, 1), 0) == block - 1
    tile = 256
    for start in range(0, width, tile):
        cols = slice(start, start + tile)
        acc = jnp.dot(pick[...], unit_ref[:, cols], preferred_element_type=jnp.float32)
        for k in range(peers):
            rows = acc[k * block : (k + 1) * block]
            rows = jnp.where(is_hdr, hdr_ref[0:1, cols], rows)
            outs[k][:, cols] = rows.astype(jnp.bfloat16)


def leader_best_kernel(reach, cap, pos_ref, *rest):
    queries, rest = rest[:4], rest[4:]
    ups, rest = rest[: reach - 1], rest[reach - 1 :]
    downs, rest = rest[: reach - 1], rest[reach - 1 :]
    outs, (q, c, q_hdr, c_hdr, sem) = rest[:4], rest[4:]
    pos = pos_ref[0]

    def copies(src, index, rows, hdrs, which):
        return [
            pltpu.make_async_copy(src.at[pl.ds(0, cap), :], rows.at[pl.ds(index * cap, cap), :], sem.at[which]),
            pltpu.make_async_copy(src.at[pl.ds(cap, SUB), :], hdrs.at[pl.ds(index * SUB, SUB), :], sem.at[which + 1]),
        ]

    started = []
    for j in range(4):
        started += copies(queries[j], j, q, q_hdr, 2 * j)
    started += copies(queries[0], 0, c, c_hdr, 8)
    for copy in started:
        copy.start()
    for k in range(1, reach):
        up = copies(ups[k - 1], k, c, c_hdr, 8 + 2 * k)
        down = copies(downs[reach - k - 1], k, c, c_hdr, 8 + 2 * k)

        @pl.when(pos >= k)
        def _():
            for copy in up:
                copy.start()

        @pl.when(pos < k)
        def _():
            for copy in down:
                copy.start()

        started += up
    for copy in started:
        copy.wait()
    c_ids = [c_hdr[k * SUB : (k + 1) * SUB, :cap].astype(jnp.float32)[0:1] for k in range(reach)]
    c_col = as_column(jnp.concatenate(c_ids, axis=1))
    for j in range(4):
        q_id = q_hdr[j * SUB : (j + 1) * SUB, :cap].astype(jnp.float32)[0:1]
        scores = lax.dot_general(c[...], q[j * cap : (j + 1) * cap, :], NT, preferred_element_type=jnp.float32)
        same = c_col == q_id
        if j == 0:
            r = lax.broadcasted_iota(jnp.int32, (reach * cap, cap), 0)
            l = lax.broadcasted_iota(jnp.int32, (reach * cap, cap), 1)
            same = same & (r != l)
        outs[j][...] = jnp.max(jnp.where(same, scores, -1.0), axis=0, keepdims=True)


def block_best_kernel(peers, block, me_ref, *rest):
    mine, rest = rest[:peers], rest[peers:]
    other, rest = rest[:peers], rest[peers:]
    out, flag, (own, far, sem) = rest[0], rest[1], rest[2:]
    width = own.shape[1]
    slots = peers * block
    started = []
    for k in range(peers):
        started.append(pltpu.make_async_copy(mine[k], own.at[pl.ds(k * block, block), :], sem.at[k]))
        started.append(pltpu.make_async_copy(other[k], far.at[pl.ds(k * block, block), :], sem.at[peers + k]))
    for copy in started:
        copy.start()
    for copy in started:
        copy.wait()
    lane = lax.broadcasted_iota(jnp.int32, (1, width), 1)

    def ids_of(rows):
        total = jnp.zeros((1, width), jnp.float32)
        for k in range(peers):
            tail = rows[(k + 1) * block - SUB : (k + 1) * block, :].astype(jnp.float32)[SUB - 1 : SUB]
            inside = (lane >= k * block) & (lane < (k + 1) * block)
            total = jnp.where(inside, tail, total)
        return total

    own_ids, far_ids = ids_of(own), ids_of(far)
    is_code = functools.reduce(jnp.logical_or, [lane == k * block + block - 1 for k in range(peers)])
    my_code = own_ids[:, block - 1 : block]
    odd = jnp.where(is_code & ((own_ids != my_code) | (far_ids != my_code)), 1.0, 0.0)
    half = jnp.floor(my_code * 0.5)
    odd = jnp.maximum(jnp.max(odd, axis=1, keepdims=True), my_code - 2.0 * half)
    flag[...] = jnp.broadcast_to(odd, flag.shape)

    q_id = own_ids[:, :slots]
    best = None
    for rows, ids in ((own, own_ids), (far, far_ids)):
        scores = lax.dot_general(rows[...], own[...], NT, preferred_element_type=jnp.float32)
        same = as_column(ids)[:slots] == q_id
        if rows is own:
            r = lax.broadcasted_iota(jnp.int32, (slots, slots), 0)
            l = lax.broadcasted_iota(jnp.int32, (slots, slots), 1)
            same = same & (r != l)
        top = jnp.max(jnp.where(same, scores, -1.0), axis=0, keepdims=True)
        best = top if best is None else jnp.maximum(best, top)
    best = jnp.broadcast_to(pad_lanes(best, width), (8, width))
    pitch = out.shape[1]
    for k in range(peers):
        piece = best if k == 0 else pltpu.roll(best, width - k * block, 1)
        to = me_ref[0] - k
        to = jnp.where(to < 0, to + peers, to)
        out[pl.ds(to, 1), :] = piece[0:1, :pitch]


def final_kernel(peers, cap, info_ref, back_ref, *rest):
    leads, out = rest[:-1], rest[-1]
    count = info_ref.shape[1]
    pitch = back_ref.shape[1]
    where = info_ref[1:2, :]
    lead = functools.reduce(jnp.maximum, [ref[...] for ref in leads])
    total = jnp.zeros((1, count), jnp.float32)
    at = lax.broadcasted_iota(jnp.int32, (pitch, count), 0)
    cols = jnp.transpose(jnp.concatenate([back_ref[...]] * (8 // math.gcd(peers, 8)), axis=0))
    for h in range(peers):
        hit = at + h * pitch == where
        total += jnp.sum(jnp.where(hit, cols[:, h : h + 1], 0.0), axis=0, keepdims=True)
    at = lax.broadcasted_iota(jnp.int32, (cap, count), 0) + peers * pitch
    total += jnp.sum(jnp.where(at == where, as_column(lead), 0.0), axis=0, keepdims=True)
    out[...] = total


def call(kernel, name, outs, in_specs, out_specs, scratch=(), flops=0, nbytes=0):
    return pl.pallas_call(
        kernel,
        name=name,
        out_shape=outs,
        in_specs=in_specs,
        out_specs=out_specs,
        scratch_shapes=list(scratch),
        compiler_params=pltpu.CompilerParams(vmem_limit_bytes=VMEM_LIMIT),
        cost_estimate=pl.CostEstimate(flops=flops, bytes_accessed=nbytes, transcendentals=0),
    )


def whole_exchange(embeddings, cluster_ids):
    count, width = embeddings.shape
    peers = lax.axis_size("dp")
    slots = 2 * count // peers
    squares = jnp.sum(embeddings * embeddings, axis=1, keepdims=True)
    unit = (embeddings * lax.rsqrt(squares + 1e-06)).astype(jnp.bfloat16)
    target = cluster_ids // CL_DEV
    onehot = (target[:, None] == jnp.arange(peers, dtype=jnp.int32)[None, :]).astype(jnp.int32)
    ranking = jnp.cumsum(onehot, axis=0) - 1
    position = jnp.sum(ranking * onehot, axis=1)
    where_to = target * slots + position
    total = peers * slots
    send_rows = jnp.zeros((total, width), jnp.bfloat16).at[where_to].set(unit)
    send_ids = jnp.full((total,), -1, jnp.int32).at[where_to].set(cluster_ids)
    own_rows = lax.all_to_all(send_rows, "dp", split_axis=0, concat_axis=0, tiled=True)
    own_ids = lax.all_to_all(send_ids, "dp", split_axis=0, concat_axis=0, tiled=True)
    swap = [(0, 1), (1, 0)]
    far_rows = lax.ppermute(own_rows, "owner", swap)
    far_ids = lax.ppermute(own_ids, "owner", swap)
    block = math.gcd(total, 512)
    column_pos = jnp.arange(total, dtype=jnp.int32)

    def block_best(start):
        queries = lax.dynamic_slice_in_dim(own_rows, start, block, 0)
        query_ids = lax.dynamic_slice_in_dim(own_ids, start, block, 0)
        row_pos = start + jnp.arange(block, dtype=jnp.int32)
        tops = []
        for rows, ids, own in ((own_rows, own_ids, True), (far_rows, far_ids, False)):
            scores = lax.dot_general(queries, rows, NT, preferred_element_type=jnp.float32)
            same = (query_ids[:, None] == ids[None, :]) & (ids[None, :] >= 0)
            if own:
                same = same & (row_pos[:, None] != column_pos[None, :])
            tops.append(jnp.max(jnp.where(same, scores, jnp.float32(-1.0)), axis=1))
        return jnp.maximum(tops[0], tops[1])

    starts = jnp.arange(total // block, dtype=jnp.int32) * block
    best = lax.map(block_best, starts).reshape(peers, slots)
    returned = lax.all_to_all(best, "dp", split_axis=0, concat_axis=0, tiled=True)
    return returned.reshape(-1)[where_to]


def local(embeddings, cluster_ids):
    count, width = embeddings.shape
    peers = lax.axis_size("dp")
    groups = lax.axis_size("groups")
    cap = 2 * count // peers
    mean = -(-(count - cap) // (peers - 1))
    block = -(-(mean + 1) // SUB) * SUB
    slots = peers * block
    pitch = -(-block // LANES) * LANES
    reach = peers // 2
    bf16, f32 = jnp.bfloat16, jnp.float32
    shape = jax.ShapeDtypeStruct
    me = lax.axis_index("dp")
    me1 = me.reshape(1)

    unit, info, hdr, lead = call(
        functools.partial(lead_kernel, peers, cap, block),
        "lead",
        [shape((count, width), bf16), shape((8, count), jnp.int32), shape((8, width), f32), shape((cap + SUB, width), bf16)],
        [SMEM, VMEM, VMEM],
        [VMEM] * 4,
        flops=2 * cap * count * width,
        nbytes=6 * count * width,
    )(me1, cluster_ids.reshape(1, count), embeddings)

    def dp_pairs(step):
        pairs = []
        for z in range(reach):
            for y in range(2):
                to = step(z, y)
                if to is not None:
                    pairs.append((2 * z + y, 2 * to[0] + to[1]))
        return pairs

    other_y = dp_pairs(lambda z, y: (z, 1 - y))
    up_pairs = dp_pairs(lambda z, y: (z + 1, y) if z + 1 < reach else None)
    down_pairs = dp_pairs(lambda z, y: (z - 1, y) if z > 0 else None)
    swap = [(0, 1), (1, 0)]

    ups, downs = [], []
    up, down = lead, lead
    for _ in range(reach - 1):
        up = lax.ppermute(up, "dp", up_pairs)
        down = lax.ppermute(down, "dp", down_pairs)
        ups.append(up)
        downs.append(down)
    blocks = call(
        functools.partial(pack_kernel, peers, block),
        "pack",
        [shape((block, width), bf16)] * peers,
        [VMEM] * 3,
        [VMEM] * peers,
        [pltpu.VMEM((slots, count), bf16)],
        flops=2 * slots * count * width,
        nbytes=4 * count * width,
    )(unit, info, hdr)
    got = [blocks[0]]
    for k in range(1, peers):
        got.append(lax.ppermute(blocks[k], "dp", [(d, (d + k) % peers) for d in range(peers)]))
    far = [lax.ppermute(rows, "owner", swap) for rows in got]

    lead_y = lax.ppermute(lead, "dp", other_y)
    lead_o = lax.ppermute(lead, "owner", swap)
    lead_yo = lax.ppermute(lead_y, "owner", swap)
    tops = call(
        functools.partial(leader_best_kernel, reach, cap),
        "leader_best",
        [shape((1, cap), f32)] * 4,
        [SMEM] + [ANY] * (4 + 2 * (reach - 1)),
        [VMEM] * 4,
        [
            pltpu.VMEM((4 * cap, width), bf16),
            pltpu.VMEM((reach * cap, width), bf16),
            pltpu.VMEM((4 * SUB, width), bf16),
            pltpu.VMEM((reach * SUB, width), bf16),
            pltpu.SemaphoreType.DMA((8 + 2 * reach,)),
        ],
        flops=8 * cap * cap * reach * width,
        nbytes=2 * (4 + reach) * cap * width,
    )((me // 2).reshape(1), lead, lead_y, lead_o, lead_yo, *ups, *downs)
    tops = [
        tops[0],
        lax.ppermute(tops[1], "dp", other_y),
        lax.ppermute(tops[2], "owner", swap),
        lax.ppermute(lax.ppermute(tops[3], "owner", swap), "dp", other_y),
    ]

    best, flag = call(
        functools.partial(block_best_kernel, peers, block),
        "block_best",
        [shape((peers, pitch), f32), shape((8, LANES), f32)],
        [SMEM] + [ANY] * (2 * peers),
        [VMEM] * 2,
        [pltpu.VMEM((slots, width), bf16), pltpu.VMEM((slots, width), bf16), pltpu.SemaphoreType.DMA((2 * peers,))],
        flops=4 * slots * slots * width,
        nbytes=4 * slots * width,
    )(me1, *got, *far)
    back = lax.all_to_all(best, "dp", split_axis=0, concat_axis=0, tiled=True)
    flags = [flag]
    for k in range(1, groups):
        flags.append(lax.ppermute(flag, "groups", [(g, (g + k) % groups) for g in range(groups)]))
    odd = functools.reduce(jnp.maximum, flags)[0, 0]
    nearest = call(
        functools.partial(final_kernel, peers, cap),
        "final",
        shape((1, count), f32),
        [VMEM] * 6,
        VMEM,
        flops=0,
        nbytes=4 * count,
    )(info, back, *tops).reshape(count)
    return lax.cond(odd > 0, whole_exchange, lambda e, c: nearest, embeddings, cluster_ids)


def solution(mesh):
    return jax.shard_map(
        local,
        mesh=mesh,
        in_specs=(P(("groups", "dp", "owner"), None), P(("groups", "dp", "owner"))),
        out_specs=P(("groups", "dp", "owner")),
        check_vma=False,
    )
```

```python
import functools
import math

import jax
import jax.numpy as jnp
from jax import lax
from jax.experimental import pallas as pl
from jax.experimental.pallas import tpu as pltpu
from jax.sharding import PartitionSpec as P

CL_DEV = 8
LANES = 128
SUB = 16
VMEM_LIMIT = 24 * 1024 * 1024
VMEM = pl.BlockSpec(memory_space=pltpu.VMEM)
SMEM = pl.BlockSpec(memory_space=pltpu.SMEM)
NT = (((1,), (1,)), ((), ()))


def pad_lanes(row, width):
    extra = width - row.shape[1]
    if extra == 0:
        return row
    return jnp.concatenate([row, jnp.zeros((row.shape[0], extra), row.dtype)], axis=1)


def as_column(row):
    return jnp.transpose(jnp.broadcast_to(row, (8, row.shape[1])))[:, 0:1]


def code_of(leader, bad):
    return 16 + 2 * leader + bad


def lead_kernel(peers, cap, block, me_ref, ids_ref, emb_ref, unit_ref, info_ref, hdr_ref, lead_ref):
    count, width = emb_ref.shape
    ids = ids_ref[...]
    target = jnp.right_shift(ids, int(math.log2(CL_DEV)))
    local_id = jnp.bitwise_and(ids, CL_DEV - 1)
    tio = lax.broadcasted_iota(jnp.int32, (peers, 1), 0)
    onehot = (lax.broadcasted_iota(jnp.int32, (peers, count), 0) == target).astype(jnp.int32)
    lane = lax.broadcasted_iota(jnp.int32, (peers, count), 1)
    cum = onehot
    step = 1
    while step < count:
        cum = cum + jnp.where(lane >= step, pltpu.roll(cum, step, 1), 0)
        step *= 2
    rank = jnp.sum(cum * onehot, axis=0, keepdims=True) - 1
    counts = cum[:, count - 1 : count]
    leader = jnp.min(jnp.where(counts == cap, tio, peers - 1), axis=0, keepdims=True)
    others = jnp.max(jnp.where(tio == leader, cap - counts, counts), axis=0, keepdims=True)
    lead_short = jnp.max(jnp.where(tio == leader, cap - counts, 0), axis=0, keepdims=True)
    bad = ((others > block - 1) | (lead_short != 0)).astype(jnp.int32)
    is_lead = target == leader
    slots = peers * block
    fits = rank < block - 1
    reach = peers // 2
    shift = jnp.right_shift(target, 1) - me_ref[0] // 2
    shift = jnp.where(shift < 0, shift + reach, shift)
    place = jnp.where(jnp.bitwise_and(target, 1) == me_ref[0] % 2, shift, reach + shift)
    dest = jnp.where(is_lead, slots + rank, jnp.where(fits, place * block + rank, -1))
    pitch = -(-block // LANES) * LANES
    final = jnp.where(is_lead, peers * pitch + rank, target * pitch + rank)
    row8 = lax.broadcasted_iota(jnp.int32, (8, count), 0)
    info_ref[...] = jnp.where(row8 == 0, dest, final)

    both = jnp.where(row8 == 0, dest, local_id + 1).astype(jnp.float32)
    both = jnp.transpose(both)
    dest_col, id_col = both[:, 0:1], both[:, 1:2]
    pieces = []
    for start in range(0, slots + cap, LANES):
        at = (lax.broadcasted_iota(jnp.int32, (count, LANES), 1) + start).astype(jnp.float32)
        pieces.append(jnp.sum(jnp.where(dest_col == at, id_col, 0.0), axis=0, keepdims=True))
    ids_at = jnp.concatenate(pieces, axis=1)
    block_ids = ids_at[:, :slots]
    slot_lane = lax.broadcasted_iota(jnp.int32, (1, slots), 1)
    last = functools.reduce(jnp.logical_or, [slot_lane == k * block + block - 1 for k in range(peers)])
    code = code_of(leader, bad).astype(jnp.float32)
    block_ids = jnp.where(last, code, block_ids)
    hdr_ref[...] = jnp.broadcast_to(pad_lanes(block_ids, width), (8, width))

    emb = emb_ref[...]
    squares = jnp.sum(emb * emb, axis=1, keepdims=True)
    unit = (emb * lax.rsqrt(squares + 1e-06)).astype(jnp.bfloat16)
    unit_ref[...] = unit
    at = lax.broadcasted_iota(jnp.int32, (cap, count), 0) + slots
    pick = jnp.where(at == dest, 1.0, 0.0).astype(jnp.bfloat16)
    lead_ref[:cap, :] = jnp.dot(pick, unit, preferred_element_type=jnp.float32).astype(jnp.bfloat16)
    lead_hdr = pad_lanes(ids_at[:, slots:], width)
    lead_ref[cap:, :] = jnp.broadcast_to(lead_hdr, (SUB, width)).astype(jnp.bfloat16)


def pack_kernel(peers, block, unit_ref, info_ref, hdr_ref, *rest):
    reach = peers // 2
    straight, across, pick = rest[:reach], rest[reach], rest[reach + 1]
    count, width = unit_ref.shape
    dest = info_ref[0:1, :]
    at = lax.broadcasted_iota(jnp.int32, (peers * block, count), 0)
    pick[...] = jnp.where(at == dest, 1.0, 0.0).astype(jnp.bfloat16)
    is_hdr = lax.broadcasted_iota(jnp.int32, (block, 1), 0) == block - 1
    tile = 256
    for start in range(0, width, tile):
        cols = slice(start, start + tile)
        acc = jnp.dot(pick[...], unit_ref[:, cols], preferred_element_type=jnp.float32)
        for k in range(peers):
            rows = acc[k * block : (k + 1) * block]
            rows = jnp.where(is_hdr, hdr_ref[0:1, cols], rows).astype(jnp.bfloat16)
            if k < reach:
                straight[k][:, cols] = rows
            else:
                across[(k - reach) * block : (k - reach + 1) * block, cols] = rows


def relay_kernel(peers, block, lead_rows, me_ref, own_up, own_down, across, lead, lead_up, lead_down, *outs):
    reach = peers // 2
    up, down, ends, queries, near = outs[:5]
    far = outs[5:]
    z = me_ref[0] // 2
    up[:lead_rows, :] = lead_up[...]
    up[lead_rows : lead_rows + block, :] = own_up[...]
    up[lead_rows + block :, :] = across[block : 2 * block, :]
    down[:lead_rows, :] = lead_down[...]
    down[lead_rows : lead_rows + block, :] = own_down[...]
    down[lead_rows + block :, :] = across[(reach - 1) * block :, :]
    for s in range(2, reach - 1):
        far[s - 2][...] = across[s * block : (s + 1) * block, :]
    queries[:lead_rows, :] = lead[...]
    for k, rows in enumerate((lead, lead_up, lead_down)):
        near[k * lead_rows : (k + 1) * lead_rows, :] = rows[...]

    def put(rows, straight, start):
        ends[:block, :] = straight[...]
        ends[block:, :] = across[start : start + block, :]

    pl.when(z == reach - 1)(functools.partial(put, ends, own_up, block))
    pl.when(z != reach - 1)(functools.partial(put, ends, own_down, (reach - 1) * block))

    def keep(rows):
        queries[lead_rows:, :] = rows[...]

    pl.when(z < reach // 2)(functools.partial(keep, lead_up))
    pl.when(z >= reach // 2)(functools.partial(keep, lead_down))


def collect_kernel(peers, block, lead_rows, me_ref, mine, across, up, down, ends, *rest):
    reach = peers // 2
    far, far_across, own = rest[: reach - 3], rest[reach - 3 : 2 * reach - 6], rest[-1]
    rest = rest[2 * reach - 6 : -1]
    count = len(rest) // 2
    z = me_ref[0] // 2
    skip = lead_rows

    def keep(slot, src):
        at = peers * block + slot * lead_rows
        own[at : at + lead_rows, :] = src[:lead_rows, :]

    for slot in range(count):
        k = slot + 2 if slot < reach - 3 else reach - 1
        pl.when(z >= k)(functools.partial(keep, slot, rest[slot]))
        pl.when(z < k)(functools.partial(keep, slot, rest[count + slot]))

    def put(k, src, start=0):
        own[k * block : (k + 1) * block, :] = src[start : start + block, :]

    def put_two(k, src, start):
        put(k, src, start)
        put(reach + k, src, start + block)

    put(0, mine)
    put(reach, across)
    for s in range(2, reach - 1):
        put(s, far[s - 2])
        put(reach + s, far_across[s - 2])
    for slot, src, missing in ((1, up, 0), (reach - 1, down, reach - 1)):
        pl.when(z == missing)(functools.partial(put_two, slot, ends, 0))
        pl.when(z != missing)(functools.partial(put_two, slot, src, skip))


def lead_ids(rows, start, cap):
    return rows[start + cap : start + cap + SUB, :cap].astype(jnp.float32)[0:1]


def lead_column(rows, start, count, cap):
    gap = jnp.zeros((SUB, 1), jnp.float32)
    parts = []
    for k in range(count):
        parts += [as_column(lead_ids(rows, start + k * (cap + SUB), cap)), gap]
    return jnp.concatenate(parts, axis=0)


def lead_tops(columns, column_ids, queries, start, cap, diagonal):
    rows = queries[start : start + cap, :]
    scores = lax.dot_general(columns, rows, NT, preferred_element_type=jnp.float32)
    same = column_ids == lead_ids(queries, start, cap)
    if diagonal:
        r = lax.broadcasted_iota(jnp.int32, scores.shape, 0)
        l = lax.broadcasted_iota(jnp.int32, scores.shape, 1)
        same = same & (r != l)
    return jnp.max(jnp.where(same, scores, -1.0), axis=0, keepdims=True)


def lead_best_kernel(slots, cap, asked, asked_y, near, near_other, own, top):
    lead_rows = cap + SUB
    count = (own.shape[0] - slots) // lead_rows
    near_ids, other_ids = lead_column(near, 0, 3, cap), lead_column(near_other, 0, 3, cap)
    far_ids = lead_column(own, slots, count, cap)
    top[...] = jnp.full(top.shape, -1.0, jnp.float32)
    for i, queries in enumerate((asked, asked_y)):
        best = lead_tops(near[...], near_ids, queries, 0, cap, i == 0)
        best = jnp.maximum(best, lead_tops(near_other[...], other_ids, queries, 0, cap, False))
        best = jnp.maximum(best, lead_tops(own[slots:, :], far_ids, queries, 0, cap, False))
        top[i : i + 1, :] = best
        top[2 + i : 3 + i, :] = lead_tops(own[slots:, :], far_ids, queries, lead_rows, cap, False)


def ids_of(rows, peers, block):
    width = rows.shape[1]
    lane = lax.broadcasted_iota(jnp.int32, (1, width), 1)
    total = jnp.zeros((1, width), jnp.float32)
    for k in range(peers):
        tail = rows[(k + 1) * block - SUB : (k + 1) * block, :].astype(jnp.float32)[SUB - 1 : SUB]
        total = jnp.where((lane >= k * block) & (lane < (k + 1) * block), tail, total)
    return total


def tops_of(rows, ids, queries, q_ids, diagonal, tile):
    slots = q_ids.shape[1]
    column = as_column(ids)[:slots]
    tops = []
    for start in range(0, slots, tile):
        stop = min(start + tile, slots)
        scores = lax.dot_general(rows[:slots, :], queries[start:stop, :], NT, preferred_element_type=jnp.float32)
        same = column == q_ids[:, start:stop]
        if diagonal:
            r = lax.broadcasted_iota(jnp.int32, scores.shape, 0)
            l = lax.broadcasted_iota(jnp.int32, scores.shape, 1) + start
            same = same & (r != l)
        tops.append(jnp.max(jnp.where(same, scores, -1.0), axis=0, keepdims=True))
    return jnp.concatenate(tops, axis=1)


def own_best_kernel(peers, block, own, top):
    slots = peers * block
    ids = ids_of(own, peers, block)
    top[0:1, :] = tops_of(own, ids, own, ids[:, :slots], True, 256)
    top[1:2, :] = ids[:, :slots]


def far_best_kernel(peers, block, edges, me_ref, own, far, top, asked, asked_y, lead_top, out, flag):
    width = own.shape[1]
    slots = peers * block
    own_ids, far_ids = top[1:2, :], ids_of(far, peers, block)
    lane = lax.broadcasted_iota(jnp.int32, (1, slots), 1)
    is_code = functools.reduce(jnp.logical_or, [lane == k * block + block - 1 for k in range(peers)])
    my_code = own_ids[:, block - 1 : block]
    odd = jnp.where(is_code & ((own_ids != my_code) | (far_ids[:, :slots] != my_code)), 1.0, 0.0)
    half = jnp.floor(my_code * 0.5)
    odd = jnp.maximum(jnp.max(odd, axis=1, keepdims=True), my_code - 2.0 * half)
    flag[...] = jnp.broadcast_to(odd, flag.shape)
    best = jnp.maximum(top[0:1, :], tops_of(far, far_ids, own, own_ids, False, 256))
    best = jnp.broadcast_to(pad_lanes(best, width), (8, width))
    reach = peers // 2
    pitch = -(-block // LANES) * LANES
    cap = out.shape[2] - pitch
    z, y = me_ref[0] // 2, me_ref[0] % 2
    none = jnp.full((1, cap), -1.0, jnp.float32)
    for k in range(peers):
        piece = best if k == 0 else pltpu.roll(best, width - k * block, 1)
        row = z - k % reach
        row = 2 * jnp.where(row < 0, row + reach, row) + (y if k < reach else 1 - y)
        out[row, :, :pitch] = piece[0:1, :pitch]
        out[k, :, pitch:] = none
    count = (far.shape[0] - slots) // (cap + SUB)
    ids = lead_column(far, slots, count, cap)
    lead = []
    for i, (queries, start) in enumerate(((asked, 0), (asked_y, 0), (asked, cap + SUB), (asked_y, cap + SUB))):
        late = lead_tops(far[slots:, :], ids, queries, start, cap, False)
        lead.append(jnp.maximum(lead_top[i : i + 1, :], late))
    out[2 * z + y, :, pitch:] = lead[0]
    out[2 * z + 1 - y, :, pitch:] = lead[1]
    if edges:
        for at, to in ((1, 0), (reach - 2, reach - 1)):

            @pl.when(z == at)
            def _():
                out[2 * to + y, :, pitch:] = lead[2]
                out[2 * to + 1 - y, :, pitch:] = lead[3]


def final_kernel(peers, cap, info_ref, back_ref, out):
    count = info_ref.shape[1]
    pitch = back_ref.shape[2] - cap
    where = info_ref[1:2, :]
    rows = [back_ref[h] for h in range(peers)]
    lead = functools.reduce(jnp.maximum, [row[:, pitch:] for row in rows])
    total = jnp.zeros((1, count), jnp.float32)
    at = lax.broadcasted_iota(jnp.int32, (pitch, count), 0)
    cols = jnp.transpose(jnp.concatenate([row[:, :pitch] for row in rows], axis=0))
    for h in range(peers):
        hit = at + h * pitch == where
        total += jnp.sum(jnp.where(hit, cols[:, h : h + 1], 0.0), axis=0, keepdims=True)
    at = lax.broadcasted_iota(jnp.int32, (cap, count), 0) + peers * pitch
    total += jnp.sum(jnp.where(at == where, as_column(lead), 0.0), axis=0, keepdims=True)
    out[...] = total


def call(kernel, name, outs, in_specs, out_specs, scratch=(), flops=0, nbytes=0):
    return pl.pallas_call(
        kernel,
        name=name,
        out_shape=outs,
        in_specs=in_specs,
        out_specs=out_specs,
        scratch_shapes=list(scratch),
        compiler_params=pltpu.CompilerParams(vmem_limit_bytes=VMEM_LIMIT),
        cost_estimate=pl.CostEstimate(flops=flops, bytes_accessed=nbytes, transcendentals=0),
    )


def whole_exchange(embeddings, cluster_ids):
    count, width = embeddings.shape
    peers = lax.axis_size("dp")
    slots = 2 * count // peers
    squares = jnp.sum(embeddings * embeddings, axis=1, keepdims=True)
    unit = (embeddings * lax.rsqrt(squares + 1e-06)).astype(jnp.bfloat16)
    target = cluster_ids // CL_DEV
    onehot = (target[:, None] == jnp.arange(peers, dtype=jnp.int32)[None, :]).astype(jnp.int32)
    ranking = jnp.cumsum(onehot, axis=0) - 1
    position = jnp.sum(ranking * onehot, axis=1)
    where_to = target * slots + position
    total = peers * slots
    send_rows = jnp.zeros((total, width), jnp.bfloat16).at[where_to].set(unit)
    send_ids = jnp.full((total,), -1, jnp.int32).at[where_to].set(cluster_ids)
    own_rows = lax.all_to_all(send_rows, "dp", split_axis=0, concat_axis=0, tiled=True)
    own_ids = lax.all_to_all(send_ids, "dp", split_axis=0, concat_axis=0, tiled=True)
    swap = [(0, 1), (1, 0)]
    far_rows = lax.ppermute(own_rows, "owner", swap)
    far_ids = lax.ppermute(own_ids, "owner", swap)
    block = math.gcd(total, 512)
    column_pos = jnp.arange(total, dtype=jnp.int32)

    def block_best(start):
        queries = lax.dynamic_slice_in_dim(own_rows, start, block, 0)
        query_ids = lax.dynamic_slice_in_dim(own_ids, start, block, 0)
        row_pos = start + jnp.arange(block, dtype=jnp.int32)
        tops = []
        for rows, ids, own in ((own_rows, own_ids, True), (far_rows, far_ids, False)):
            scores = lax.dot_general(queries, rows, NT, preferred_element_type=jnp.float32)
            same = (query_ids[:, None] == ids[None, :]) & (ids[None, :] >= 0)
            if own:
                same = same & (row_pos[:, None] != column_pos[None, :])
            tops.append(jnp.max(jnp.where(same, scores, jnp.float32(-1.0)), axis=1))
        return jnp.maximum(tops[0], tops[1])

    starts = jnp.arange(total // block, dtype=jnp.int32) * block
    best = lax.map(block_best, starts).reshape(peers, slots)
    returned = lax.all_to_all(best, "dp", split_axis=0, concat_axis=0, tiled=True)
    return returned.reshape(-1)[where_to]


def local(embeddings, cluster_ids):
    count, width = embeddings.shape
    peers = lax.axis_size("dp")
    groups = lax.axis_size("groups")
    cap = 2 * count // peers
    mean = -(-(count - cap) // (peers - 1))
    block = -(-(mean + 1) // SUB) * SUB
    slots = peers * block
    pitch = -(-block // LANES) * LANES
    reach = peers // 2
    bf16, f32 = jnp.bfloat16, jnp.float32
    shape = jax.ShapeDtypeStruct
    me = lax.axis_index("dp")
    me1 = me.reshape(1)

    unit, info, hdr, lead = call(
        functools.partial(lead_kernel, peers, cap, block),
        "lead",
        [shape((count, width), bf16), shape((8, count), jnp.int32), shape((8, width), f32), shape((cap + SUB, width), bf16)],
        [SMEM, VMEM, VMEM],
        [VMEM] * 4,
        flops=2 * cap * count * width,
        nbytes=6 * count * width,
    )(me1, cluster_ids.reshape(1, count), embeddings)

    def dp_pairs(step):
        pairs = []
        for z in range(reach):
            for y in range(2):
                to = step(z, y)
                if to is not None:
                    pairs.append((2 * z + y, 2 * to[0] + to[1]))
        return pairs

    other_y = dp_pairs(lambda z, y: (z, 1 - y))
    up_pairs = dp_pairs(lambda z, y: (z + 1, y) if z + 1 < reach else None)
    down_pairs = dp_pairs(lambda z, y: (z - 1, y) if z > 0 else None)
    swap = [(0, 1), (1, 0)]

    ends_pairs = dp_pairs(lambda z, y: (reach - 1 - z, y) if z in (0, reach - 1) else None)
    shift_pairs = [dp_pairs(lambda z, y, s=s: ((z + s) % reach, y)) for s in range(2, reach - 1)]

    one = shape((block, width), bf16)
    two = shape((2 * block, width), bf16)
    lead_rows = cap + SUB
    message = shape((lead_rows + 2 * block, width), bf16)
    edges = reach == 4

    up1 = lax.ppermute(lead, "dp", up_pairs)
    down1 = lax.ppermute(lead, "dp", down_pairs)
    *straight, across = call(
        functools.partial(pack_kernel, peers, block),
        "pack",
        [one] * reach + [shape((reach * block, width), bf16)],
        [VMEM] * 3,
        [VMEM] * (reach + 1),
        [pltpu.VMEM((slots, count), bf16)],
        flops=2 * slots * count * width,
        nbytes=4 * count * width,
    )(unit, info, hdr)
    across = lax.ppermute(across, "dp", other_y)
    fars = [lax.ppermute(straight[s + 2], "dp", pairs) for s, pairs in enumerate(shift_pairs)]
    across, fars, up1, down1 = lax.optimization_barrier((across, fars, up1, down1))
    up2, down2, ends, asked, near, *fars_r = call(
        functools.partial(relay_kernel, peers, block, lead_rows),
        "relay",
        [message, message, two, shape((2 * lead_rows, width), bf16), shape((3 * lead_rows, width), bf16)] + [one] * (reach - 3),
        [SMEM] + [VMEM] * 6,
        [VMEM] * (2 + reach),
        nbytes=2 * slots * width,
    )(me1, straight[1], straight[reach - 1], across, lead, up1, down1)
    up2 = lax.ppermute(up2, "dp", up_pairs)
    down2 = lax.ppermute(down2, "dp", down_pairs)
    ends = lax.ppermute(ends, "dp", ends_pairs)
    fars_r = [lax.ppermute(rows, "dp", pairs) for rows, pairs in zip(fars_r, shift_pairs)]
    asked_y = lax.ppermute(asked, "dp", other_y)
    up2, down2, ends, fars_r, asked_y, near = lax.optimization_barrier((up2, down2, ends, fars_r, asked_y, near))
    near_o = lax.ppermute(near, "owner", swap)
    ups, downs = [up2], [down2]
    if not edges:
        up, down = up2[:lead_rows], down2[:lead_rows]
        for _ in range(reach - 3):
            up = lax.ppermute(up, "dp", up_pairs)
            down = lax.ppermute(down, "dp", down_pairs)
            ups.append(up)
            downs.append(down)
        ups, downs = ups[:-1] + ups[-1:], downs[:-1][::-1] + downs[-1:]

    n_late = len(ups)
    own = call(
        functools.partial(collect_kernel, peers, block, lead_rows),
        "collect",
        shape((slots + n_late * lead_rows, width), bf16),
        [SMEM] + [VMEM] * (5 + 2 * (reach - 3) + 2 * n_late),
        VMEM,
        nbytes=4 * slots * width,
    )(me1, straight[0], across, up2, down2, ends, *fars, *fars_r, *ups, *downs)
    far = lax.ppermute(own, "owner", swap)
    lead_top = call(
        functools.partial(lead_best_kernel, slots, cap),
        "lead_best",
        shape((8, cap), f32),
        [VMEM] * 5,
        VMEM,
        flops=4 * (6 + 2 * n_late) * cap * cap * width,
        nbytes=2 * (10 + n_late) * cap * width,
    )(asked, asked_y, near, near_o, own)
    top = call(
        functools.partial(own_best_kernel, peers, block),
        "own_best",
        shape((8, slots), f32),
        [VMEM],
        VMEM,
        flops=2 * slots * slots * width,
        nbytes=2 * slots * width,
    )(own)
    best, flag = call(
        functools.partial(far_best_kernel, peers, block, edges),
        "far_best",
        [shape((peers, 1, pitch + cap), f32), shape((8, LANES), f32)],
        [SMEM] + [VMEM] * 6,
        [VMEM] * 2,
        flops=2 * slots * slots * width + 8 * n_late * cap * cap * width,
        nbytes=4 * slots * width,
    )(me1, own, far, top, asked, asked_y, lead_top)
    back = lax.all_to_all(best, "dp", split_axis=0, concat_axis=0, tiled=True)
    flags = [flag]
    for k in range(1, groups):
        flags.append(lax.ppermute(flag, "groups", [(g, (g + k) % groups) for g in range(groups)]))
    odd = functools.reduce(jnp.maximum, flags)[0, 0]
    nearest = call(
        functools.partial(final_kernel, peers, cap),
        "final",
        shape((1, count), f32),
        [VMEM] * 2,
        VMEM,
        flops=0,
        nbytes=4 * count,
    )(info, back).reshape(count)
    return lax.cond(odd > 0, whole_exchange, lambda e, c: nearest, embeddings, cluster_ids)


def solution(mesh):
    return jax.shard_map(
        local,
        mesh=mesh,
        in_specs=(P(("groups", "dp", "owner"), None), P(("groups", "dp", "owner"))),
        out_specs=P(("groups", "dp", "owner")),
        check_vma=False,
    )
```

```python
import functools
import math

import jax
import jax.numpy as jnp
from jax import lax
from jax.experimental import pallas as pl
from jax.experimental.pallas import tpu as pltpu
from jax.sharding import PartitionSpec as P

CL_DEV = 8
LANES = 128
CHUNKS = 4
SUB = 16
VMEM_LIMIT = 14 * 1024 * 1024
VMEM = pl.BlockSpec(memory_space=pltpu.VMEM)
SMEM = pl.BlockSpec(memory_space=pltpu.SMEM)
NT = (((1,), (1,)), ((), ()))


def pad_lanes(row, width):
    extra = width - row.shape[1]
    if extra == 0:
        return row
    return jnp.concatenate([row, jnp.zeros((row.shape[0], extra), row.dtype)], axis=1)


def as_column(row):
    return jnp.transpose(jnp.broadcast_to(row, (8, row.shape[1])))[:, 0:1]


def code_of(leader, bad):
    return 16 + 2 * leader + bad


def pack_kernel(peers, cap, block, me_ref, ids_ref, emb_hbm, info_ref, mine, mine_across, lead, near, odd, across, *rest):
    far, (emb_ref, unit_ref, pick, sem) = rest[:-4], rest[-4:]
    count, width = emb_ref.shape
    chunk = count // CHUNKS
    copies = []
    for i in range(CHUNKS):
        rows = pl.ds(i * chunk, chunk)
        copies.append(pltpu.make_async_copy(emb_hbm.at[rows, :], emb_ref.at[rows, :], sem.at[i]))
        copies[-1].start()
    ids = ids_ref[...]
    target = jnp.right_shift(ids, int(math.log2(CL_DEV)))
    local_id = jnp.bitwise_and(ids, CL_DEV - 1)
    tio = lax.broadcasted_iota(jnp.int32, (peers, 1), 0)
    onehot = (lax.broadcasted_iota(jnp.int32, (peers, count), 0) == target).astype(jnp.int32)
    lane = lax.broadcasted_iota(jnp.int32, (peers, count), 1)
    cum = onehot
    step = 1
    while step < count:
        cum = cum + jnp.where(lane >= step, pltpu.roll(cum, step, 1), 0)
        step *= 2
    rank = jnp.sum(cum * onehot, axis=0, keepdims=True) - 1
    counts = cum[:, count - 1 : count]
    leader = jnp.min(jnp.where(counts == cap, tio, peers - 1), axis=0, keepdims=True)
    others = jnp.max(jnp.where(tio == leader, cap - counts, counts), axis=0, keepdims=True)
    lead_short = jnp.max(jnp.where(tio == leader, cap - counts, 0), axis=0, keepdims=True)
    bad = ((others > block - 1) | (lead_short != 0)).astype(jnp.int32)
    is_lead = target == leader
    slots = peers * block
    fits = rank < block - 1
    reach = peers // 2
    z = me_ref[0] // 2
    shift = jnp.right_shift(target, 1) - z
    shift = jnp.where(z % 2 == 0, shift, -shift)
    shift = jnp.where(shift < 0, shift + reach, shift)
    place = jnp.where(jnp.bitwise_and(target, 1) == me_ref[0] % 2, shift, reach + shift)
    dest = jnp.where(is_lead, slots + rank, jnp.where(fits, place * block + rank, -1))
    pitch = -(-block // LANES) * LANES
    final = jnp.where(is_lead, peers * pitch + rank, target * pitch + rank)
    row8 = lax.broadcasted_iota(jnp.int32, (8, count), 0)
    info_ref[...] = jnp.where(row8 == 0, dest, final)

    both = jnp.where(row8 == 0, dest, local_id + 1).astype(jnp.float32)
    both = jnp.transpose(both)
    dest_col, id_col = both[:, 0:1], both[:, 1:2]
    pieces = []
    for start in range(0, slots + cap, LANES):
        at = (lax.broadcasted_iota(jnp.int32, (count, LANES), 1) + start).astype(jnp.float32)
        pieces.append(jnp.sum(jnp.where(dest_col == at, id_col, 0.0), axis=0, keepdims=True))
    ids_at = jnp.concatenate(pieces, axis=1)
    block_ids = ids_at[:, :slots]
    slot_lane = lax.broadcasted_iota(jnp.int32, (1, slots), 1)
    last = functools.reduce(jnp.logical_or, [slot_lane == k * block + block - 1 for k in range(peers)])
    code = code_of(leader, bad).astype(jnp.float32)
    block_ids = jnp.where(last, code, block_ids)
    hdr = pad_lanes(block_ids, width)
    lead_hdr = jnp.broadcast_to(pad_lanes(ids_at[:, slots:], width), (SUB, width)).astype(jnp.bfloat16)
    lead[cap:, :] = lead_hdr
    odd[cap : cap + SUB, :] = lead_hdr
    at = lax.broadcasted_iota(jnp.int32, (slots + cap, count), 0)
    pick[...] = jnp.where(at == dest, 1.0, 0.0).astype(jnp.bfloat16)

    for i in range(CHUNKS):
        copies[i].wait()
        rows = slice(i * chunk, (i + 1) * chunk)
        emb = emb_ref[rows, :]
        squares = jnp.sum(emb * emb, axis=1, keepdims=True)
        unit_ref[rows, :] = (emb * lax.rsqrt(squares + 1e-06)).astype(jnp.bfloat16)

    places = [(mine, 0), (near, 0), *[(ref, 0) for ref in far], (odd, cap + SUB), (mine_across, 0)]
    places += [(across, s * block) for s in range(reach - 1)]
    is_hdr = lax.broadcasted_iota(jnp.int32, (block, 1), 0) == block - 1
    tile = 256
    for start in range(0, width, tile):
        cols = slice(start, start + tile)
        acc = jnp.dot(pick[...], unit_ref[:, cols], preferred_element_type=jnp.float32)
        for k, (ref, at) in enumerate(places):
            rows = acc[k * block : (k + 1) * block]
            ref[at : at + block, cols] = jnp.where(is_hdr, hdr[:, cols], rows).astype(jnp.bfloat16)
        lead[:cap, cols] = acc[slots:].astype(jnp.bfloat16)
        odd[:cap, cols] = acc[slots:].astype(jnp.bfloat16)


def relay_kernel(peers, block, lead_rows, lead, near, odd, mine_across, across, lead_even, lead_odd, *outs):
    reach = peers // 2
    even_out, odd_out, ends, queries = outs[:4]
    far = outs[4:]
    last = (reach - 2) * block
    even_out[:lead_rows, :] = lead_odd[:lead_rows, :]
    even_out[lead_rows : lead_rows + block, :] = near[...]
    even_out[lead_rows + block :, :] = across[:block, :]
    odd_out[:lead_rows, :] = lead_even[...]
    odd_out[lead_rows:, :] = across[last:, :]
    ends[:block, :] = odd[lead_rows:, :]
    ends[block:, :] = across[last:, :]
    for s in range(2, reach - 1):
        far[s - 2][...] = across[(s - 1) * block : s * block, :]
    queries[:lead_rows, :] = lead[...]
    queries[lead_rows : 2 * lead_rows, :] = lead_even[...]
    queries[2 * lead_rows :, :] = mine_across[...]


def collect_kernel(peers, block, lead_rows, me_ref, mine, odd, asked_y, even2, odd2, ends, lead, lead_even, *rest):
    reach = peers // 2
    far, far_across, (own, cols) = rest[: reach - 3], rest[reach - 3 : 2 * reach - 6], rest[-2:]
    rest = rest[2 * reach - 6 : -2]
    z = me_ref[0] // 2
    at_end = (z == 0) | (z == reach - 1)

    def put(k, src, start=0):
        own[k * block : (k + 1) * block, :] = src[start : start + block, :]

    def put_last(first, second, start, then):
        put(reach - 1, first, start)
        put(2 * reach - 1, second, then)

    put(0, mine)
    put(reach, asked_y, 2 * lead_rows)
    put(1, even2, lead_rows)
    put(reach + 1, even2, lead_rows + block)
    for s in range(2, reach - 1):
        put(s, far[s - 2])
        put(reach + s, far_across[s - 2])
    pl.when(at_end)(functools.partial(put_last, ends, ends, 0, block))
    pl.when(jnp.logical_not(at_end))(functools.partial(put_last, odd, odd2, lead_rows, lead_rows))

    def keep(slot, src):
        cols[slot * lead_rows : (slot + 1) * lead_rows, :] = src[:lead_rows, :]

    for slot, src in enumerate((lead, lead_even, odd)):
        keep(slot, src)
    if reach == 4:
        pl.when(at_end)(functools.partial(keep, 3, even2))
        pl.when(jnp.logical_not(at_end))(functools.partial(keep, 3, odd2))
    else:
        for slot, src in enumerate(rest):
            keep(3 + slot, src)


def lead_ids(rows, start, cap):
    return rows[start + cap : start + cap + SUB, :cap].astype(jnp.float32)[0:1]


def lead_column(rows, start, count, cap):
    gap = jnp.zeros((SUB, 1), jnp.float32)
    parts = []
    for k in range(count):
        parts += [as_column(lead_ids(rows, start + k * (cap + SUB), cap)), gap]
    return jnp.concatenate(parts, axis=0)


def lead_tops(columns, column_ids, queries, start, cap, diagonal):
    rows = queries[start : start + cap, :]
    scores = lax.dot_general(columns, rows, NT, preferred_element_type=jnp.float32)
    same = column_ids == lead_ids(queries, start, cap)
    if diagonal:
        r = lax.broadcasted_iota(jnp.int32, scores.shape, 0)
        l = lax.broadcasted_iota(jnp.int32, scores.shape, 1)
        same = same & (r != l)
    return jnp.max(jnp.where(same, scores, -1.0), axis=0, keepdims=True)


def lead_best_kernel(cap, asked, asked_y, cols, cols_other, top):
    lead_rows = cap + SUB
    count = cols.shape[0] // lead_rows
    late = 3 * lead_rows
    top[...] = jnp.full(top.shape, -1.0, jnp.float32)
    for columns in (cols, cols_other):
        ids = lead_column(columns, 0, count, cap)
        for i, queries in enumerate((asked, asked_y)):
            best = lead_tops(columns[...], ids, queries, 0, cap, i == 0 and columns is cols)
            top[i : i + 1, :] = jnp.maximum(top[i : i + 1, :], best)
            best = lead_tops(columns[late:, :], ids[late:], queries, lead_rows, cap, False)
            top[2 + i : 3 + i, :] = jnp.maximum(top[2 + i : 3 + i, :], best)


def ids_of(rows, peers, block):
    width = rows.shape[1]
    lane = lax.broadcasted_iota(jnp.int32, (1, width), 1)
    total = jnp.zeros((1, width), jnp.float32)
    for k in range(peers):
        tail = rows[(k + 1) * block - SUB : (k + 1) * block, :].astype(jnp.float32)[SUB - 1 : SUB]
        total = jnp.where((lane >= k * block) & (lane < (k + 1) * block), tail, total)
    return total


def tops_of(rows, ids, queries, q_ids, diagonal, tile):
    slots = q_ids.shape[1]
    column = as_column(ids)[:slots]
    tops = []
    for start in range(0, slots, tile):
        stop = min(start + tile, slots)
        scores = lax.dot_general(rows[:slots, :], queries[start:stop, :], NT, preferred_element_type=jnp.float32)
        same = column == q_ids[:, start:stop]
        if diagonal:
            r = lax.broadcasted_iota(jnp.int32, scores.shape, 0)
            l = lax.broadcasted_iota(jnp.int32, scores.shape, 1) + start
            same = same & (r != l)
        tops.append(jnp.max(jnp.where(same, scores, -1.0), axis=0, keepdims=True))
    return jnp.concatenate(tops, axis=1)


def own_best_kernel(peers, block, own, top):
    slots = peers * block
    ids = ids_of(own, peers, block)
    top[0:1, :] = tops_of(own, ids, own, ids[:, :slots], True, 256)
    top[1:2, :] = ids[:, :slots]


def far_best_kernel(peers, block, edges, me_ref, own, far, top, lead_top, out, flag):
    width = own.shape[1]
    slots = peers * block
    own_ids, far_ids = top[1:2, :], ids_of(far, peers, block)
    lane = lax.broadcasted_iota(jnp.int32, (1, slots), 1)
    is_code = functools.reduce(jnp.logical_or, [lane == k * block + block - 1 for k in range(peers)])
    my_code = own_ids[:, block - 1 : block]
    odd = jnp.where(is_code & ((own_ids != my_code) | (far_ids[:, :slots] != my_code)), 1.0, 0.0)
    half = jnp.floor(my_code * 0.5)
    odd = jnp.maximum(jnp.max(odd, axis=1, keepdims=True), my_code - 2.0 * half)
    flag[...] = jnp.broadcast_to(odd, flag.shape)
    best = jnp.maximum(top[0:1, :], tops_of(far, far_ids, own, own_ids, False, 256))
    best = jnp.broadcast_to(pad_lanes(best, width), (8, width))
    reach = peers // 2
    pitch = -(-block // LANES) * LANES
    cap = out.shape[2] - pitch
    z, y = me_ref[0] // 2, me_ref[0] % 2
    none = jnp.full((1, cap), -1.0, jnp.float32)
    for k in range(peers):
        piece = best if k == 0 else pltpu.roll(best, width - k * block, 1)
        up = (z % 2 == 0) == (k % 2 == 1)
        row = z + jnp.where(up, k % reach, reach - k % reach)
        row = 2 * (row % reach) + (y if k < reach else 1 - y)
        out[row, :, :pitch] = piece[0:1, :pitch]
        out[k, :, pitch:] = none
    lead = [lead_top[i : i + 1, :] for i in range(4)]
    out[2 * z + y, :, pitch:] = lead[0]
    out[2 * z + 1 - y, :, pitch:] = lead[1]
    if edges:
        for at, to in ((1, 0), (reach - 2, reach - 1)):

            @pl.when(z == at)
            def _():
                out[2 * to + y, :, pitch:] = lead[2]
                out[2 * to + 1 - y, :, pitch:] = lead[3]


def final_kernel(peers, cap, info_ref, back_ref, out):
    count = info_ref.shape[1]
    pitch = back_ref.shape[2] - cap
    where = info_ref[1:2, :]
    rows = [back_ref[h] for h in range(peers)]
    lead = functools.reduce(jnp.maximum, [row[:, pitch:] for row in rows])
    total = jnp.zeros((1, count), jnp.float32)
    at = lax.broadcasted_iota(jnp.int32, (pitch, count), 0)
    cols = jnp.transpose(jnp.concatenate([row[:, :pitch] for row in rows], axis=0))
    for h in range(peers):
        hit = at + h * pitch == where
        total += jnp.sum(jnp.where(hit, cols[:, h : h + 1], 0.0), axis=0, keepdims=True)
    at = lax.broadcasted_iota(jnp.int32, (cap, count), 0) + peers * pitch
    total += jnp.sum(jnp.where(at == where, as_column(lead), 0.0), axis=0, keepdims=True)
    out[...] = total


def call(kernel, name, outs, in_specs, out_specs, scratch=(), flops=0, nbytes=0):
    return pl.pallas_call(
        kernel,
        name=name,
        out_shape=outs,
        in_specs=in_specs,
        out_specs=out_specs,
        scratch_shapes=list(scratch),
        compiler_params=pltpu.CompilerParams(vmem_limit_bytes=VMEM_LIMIT),
        cost_estimate=pl.CostEstimate(flops=flops, bytes_accessed=nbytes, transcendentals=0),
    )


def whole_exchange(embeddings, cluster_ids):
    count, width = embeddings.shape
    peers = lax.axis_size("dp")
    slots = 2 * count // peers
    squares = jnp.sum(embeddings * embeddings, axis=1, keepdims=True)
    unit = (embeddings * lax.rsqrt(squares + 1e-06)).astype(jnp.bfloat16)
    target = cluster_ids // CL_DEV
    onehot = (target[:, None] == jnp.arange(peers, dtype=jnp.int32)[None, :]).astype(jnp.int32)
    ranking = jnp.cumsum(onehot, axis=0) - 1
    position = jnp.sum(ranking * onehot, axis=1)
    where_to = target * slots + position
    total = peers * slots
    send_rows = jnp.zeros((total, width), jnp.bfloat16).at[where_to].set(unit)
    send_ids = jnp.full((total,), -1, jnp.int32).at[where_to].set(cluster_ids)
    own_rows = lax.all_to_all(send_rows, "dp", split_axis=0, concat_axis=0, tiled=True)
    own_ids = lax.all_to_all(send_ids, "dp", split_axis=0, concat_axis=0, tiled=True)
    swap = [(0, 1), (1, 0)]
    far_rows = lax.ppermute(own_rows, "owner", swap)
    far_ids = lax.ppermute(own_ids, "owner", swap)
    block = math.gcd(total, 512)
    column_pos = jnp.arange(total, dtype=jnp.int32)

    def block_best(start):
        queries = lax.dynamic_slice_in_dim(own_rows, start, block, 0)
        query_ids = lax.dynamic_slice_in_dim(own_ids, start, block, 0)
        row_pos = start + jnp.arange(block, dtype=jnp.int32)
        tops = []
        for rows, ids, own in ((own_rows, own_ids, True), (far_rows, far_ids, False)):
            scores = lax.dot_general(queries, rows, NT, preferred_element_type=jnp.float32)
            same = (query_ids[:, None] == ids[None, :]) & (ids[None, :] >= 0)
            if own:
                same = same & (row_pos[:, None] != column_pos[None, :])
            tops.append(jnp.max(jnp.where(same, scores, jnp.float32(-1.0)), axis=1))
        return jnp.maximum(tops[0], tops[1])

    starts = jnp.arange(total // block, dtype=jnp.int32) * block
    best = lax.map(block_best, starts).reshape(peers, slots)
    returned = lax.all_to_all(best, "dp", split_axis=0, concat_axis=0, tiled=True)
    return returned.reshape(-1)[where_to]


def local(embeddings, cluster_ids):
    count, width = embeddings.shape
    peers = lax.axis_size("dp")
    groups = lax.axis_size("groups")
    cap = 2 * count // peers
    mean = -(-(count - cap) // (peers - 1))
    block = -(-(mean + 1) // SUB) * SUB
    slots = peers * block
    pitch = -(-block // LANES) * LANES
    reach = peers // 2
    bf16, f32 = jnp.bfloat16, jnp.float32
    shape = jax.ShapeDtypeStruct
    me = lax.axis_index("dp")
    me1 = me.reshape(1)

    def dp_pairs(step):
        pairs = []
        for z in range(reach):
            for y in range(2):
                to = step(z, y)
                if to is not None:
                    pairs.append((2 * z + y, 2 * to[0] + to[1]))
        return pairs

    other_y = dp_pairs(lambda z, y: (z, 1 - y))
    up_pairs = dp_pairs(lambda z, y: (z + 1, y) if z + 1 < reach else None)
    down_pairs = dp_pairs(lambda z, y: (z - 1, y) if z > 0 else None)
    swap = [(0, 1), (1, 0)]

    ends_pairs = dp_pairs(lambda z, y: (reach - 1 - z, y) if z in (0, reach - 1) else None)
    shift_pairs = [
        dp_pairs(lambda z, y, s=s: ((z + (s if z % 2 == 0 else reach - s)) % reach, y)) for s in range(2, reach - 1)
    ]
    even_pairs = dp_pairs(lambda z, y: (z ^ 1, y))
    odd_pairs = dp_pairs(lambda z, y: (((z + 1) ^ 1) - 1, y) if 0 < z < reach - 1 else None)

    one = shape((block, width), bf16)
    lead_rows = cap + SUB
    message = shape((lead_rows + block, width), bf16)
    edges = reach == 4

    info, mine, mine_across, lead, near, odd, across, *fars = call(
        functools.partial(pack_kernel, peers, cap, block),
        "pack",
        [shape((8, count), jnp.int32), one, one, shape((lead_rows, width), bf16), one, message]
        + [shape(((reach - 1) * block, width), bf16)]
        + [one] * (reach - 3),
        [SMEM, VMEM, pl.BlockSpec(memory_space=pltpu.HBM)],
        [VMEM] * (4 + reach),
        [
            pltpu.VMEM((count, width), f32),
            pltpu.VMEM((count, width), bf16),
            pltpu.VMEM((slots + cap, count), bf16),
            pltpu.SemaphoreType.DMA((CHUNKS,)),
        ],
        flops=2 * (slots + cap) * count * width,
        nbytes=8 * count * width,
    )(me1, cluster_ids.reshape(1, count), embeddings)
    odd1 = lax.ppermute(odd, "dp", odd_pairs)
    even1 = lax.ppermute(lead, "dp", even_pairs)
    across = lax.ppermute(across, "dp", other_y)
    fars = [lax.ppermute(rows, "dp", pairs) for rows, pairs in zip(fars, shift_pairs)]
    across, fars, odd1, even1 = lax.optimization_barrier((across, fars, odd1, even1))
    even2, odd2, ends, asked, *fars_r = call(
        functools.partial(relay_kernel, peers, block, lead_rows),
        "relay",
        [
            shape((lead_rows + 2 * block, width), bf16),
            message,
            shape((2 * block, width), bf16),
            shape((2 * lead_rows + block, width), bf16),
        ]
        + [one] * (reach - 3),
        [VMEM] * 7,
        [VMEM] * (1 + reach),
        nbytes=2 * slots * width,
    )(lead, near, odd, mine_across, across, even1, odd1)
    odd2 = lax.ppermute(odd2, "dp", odd_pairs)
    even2 = lax.ppermute(even2, "dp", even_pairs)
    ends = lax.ppermute(ends, "dp", ends_pairs)
    fars_r = [lax.ppermute(rows, "dp", pairs) for rows, pairs in zip(fars_r, shift_pairs)]
    asked_y = lax.ppermute(asked, "dp", other_y)
    odd2, even2, ends, fars_r, asked_y = lax.optimization_barrier((odd2, even2, ends, fars_r, asked_y))
    late = []
    if not edges:
        is_even = (me // 2) % 2 == 0
        up = jnp.where(is_even, odd2[:lead_rows], even2[:lead_rows])
        down = jnp.where(is_even, even2[:lead_rows], odd2[:lead_rows])
        late = [up, down]
        for _ in range(reach - 3):
            up = lax.ppermute(up, "dp", up_pairs)
            down = lax.ppermute(down, "dp", down_pairs)
            late += [up, down]
    own, cols = call(
        functools.partial(collect_kernel, peers, block, lead_rows),
        "collect",
        [shape((slots, width), bf16), shape(((3 + max(1, len(late))) * lead_rows, width), bf16)],
        [SMEM] + [VMEM] * (8 + 2 * (reach - 3) + len(late)),
        [VMEM] * 2,
        nbytes=4 * slots * width,
    )(me1, mine, odd1, asked_y, even2, odd2, ends, lead, even1, *fars, *fars_r, *late)
    cols_o = lax.ppermute(cols, "owner", swap)
    far = lax.ppermute(own, "owner", swap)
    lead_top = call(
        functools.partial(lead_best_kernel, cap),
        "lead_best",
        shape((8, cap), f32),
        [VMEM] * 4,
        VMEM,
        flops=40 * cap * cap * width,
        nbytes=20 * cap * width,
    )(asked, asked_y, cols, cols_o)
    top = call(
        functools.partial(own_best_kernel, peers, block),
        "own_best",
        shape((8, slots), f32),
        [VMEM],
        VMEM,
        flops=2 * slots * slots * width,
        nbytes=2 * slots * width,
    )(own)
    best, flag = call(
        functools.partial(far_best_kernel, peers, block, edges),
        "far_best",
        [shape((peers, 1, pitch + cap), f32), shape((8, LANES), f32)],
        [SMEM] + [VMEM] * 4,
        [VMEM] * 2,
        flops=2 * slots * slots * width,
        nbytes=4 * slots * width,
    )(me1, own, far, top, lead_top)
    back = lax.all_to_all(best, "dp", split_axis=0, concat_axis=0, tiled=True)
    flags = [flag]
    for k in range(1, groups):
        flags.append(lax.ppermute(flag, "groups", [(g, (g + k) % groups) for g in range(groups)]))
    odd = functools.reduce(jnp.maximum, flags)[0, 0]
    nearest = call(
        functools.partial(final_kernel, peers, cap),
        "final",
        shape((1, count), f32),
        [VMEM] * 2,
        VMEM,
        flops=0,
        nbytes=4 * count,
    )(info, back).reshape(count)
    return lax.cond(odd > 0, whole_exchange, lambda e, c: nearest, embeddings, cluster_ids)


def solution(mesh):
    return jax.shard_map(
        local,
        mesh=mesh,
        in_specs=(P(("groups", "dp", "owner"), None), P(("groups", "dp", "owner"))),
        out_specs=P(("groups", "dp", "owner")),
        check_vma=False,
    )
```

```python
import functools
import math

import jax
import jax.numpy as jnp
from jax import lax
from jax.experimental import pallas as pl
from jax.experimental.pallas import tpu as pltpu
from jax.sharding import PartitionSpec as P

CL_DEV = 8
LANES = 128
CHUNKS = 4
SUB = 16
VMEM_LIMIT = 14 * 1024 * 1024
VMEM = pl.BlockSpec(memory_space=pltpu.VMEM)
SMEM = pl.BlockSpec(memory_space=pltpu.SMEM)
NT = (((1,), (1,)), ((), ()))


def pad_lanes(row, width):
    extra = width - row.shape[1]
    if extra == 0:
        return row
    return jnp.concatenate([row, jnp.zeros((row.shape[0], extra), row.dtype)], axis=1)


def as_column(row):
    return jnp.transpose(jnp.broadcast_to(row, (8, row.shape[1])))[:, 0:1]


def code_of(leader, bad):
    return 16 + 2 * leader + bad


def pack_kernel(peers, cap, block, me_ref, ids_ref, emb_hbm, info_ref, mine, mine_across, even, odd, across, *rest):
    far, (emb_ref, unit_ref, pick, sem) = rest[:-4], rest[-4:]
    count, width = emb_ref.shape
    chunk = count // CHUNKS
    copies = []
    for i in range(CHUNKS):
        rows = pl.ds(i * chunk, chunk)
        copies.append(pltpu.make_async_copy(emb_hbm.at[rows, :], emb_ref.at[rows, :], sem.at[i]))
        copies[-1].start()
    ids = ids_ref[...]
    target = jnp.right_shift(ids, int(math.log2(CL_DEV)))
    local_id = jnp.bitwise_and(ids, CL_DEV - 1)
    tio = lax.broadcasted_iota(jnp.int32, (peers, 1), 0)
    onehot = (lax.broadcasted_iota(jnp.int32, (peers, count), 0) == target).astype(jnp.int32)
    lane = lax.broadcasted_iota(jnp.int32, (peers, count), 1)
    cum = onehot
    step = 1
    while step < count:
        cum = cum + jnp.where(lane >= step, pltpu.roll(cum, step, 1), 0)
        step *= 2
    rank = jnp.sum(cum * onehot, axis=0, keepdims=True) - 1
    counts = cum[:, count - 1 : count]
    leader = jnp.min(jnp.where(counts == cap, tio, peers - 1), axis=0, keepdims=True)
    others = jnp.max(jnp.where(tio == leader, cap - counts, counts), axis=0, keepdims=True)
    lead_short = jnp.max(jnp.where(tio == leader, cap - counts, 0), axis=0, keepdims=True)
    bad = ((others > block - 1) | (lead_short != 0)).astype(jnp.int32)
    is_lead = target == leader
    slots = peers * block
    fits = rank < block - 1
    reach = peers // 2
    z = me_ref[0] // 2
    shift = jnp.right_shift(target, 1) - z
    shift = jnp.where(z % 2 == 0, shift, -shift)
    shift = jnp.where(shift < 0, shift + reach, shift)
    place = jnp.where(jnp.bitwise_and(target, 1) == me_ref[0] % 2, shift, reach + shift)
    dest = jnp.where(is_lead, slots + rank, jnp.where(fits, place * block + rank, -1))
    pitch = -(-block // LANES) * LANES
    final = jnp.where(is_lead, peers * pitch + rank, target * pitch + rank)
    row8 = lax.broadcasted_iota(jnp.int32, (8, count), 0)
    info_ref[...] = jnp.where(row8 == 0, dest, final)

    both = jnp.where(row8 == 0, dest, local_id + 1).astype(jnp.float32)
    both = jnp.transpose(both)
    dest_col, id_col = both[:, 0:1], both[:, 1:2]
    pieces = []
    for start in range(0, slots + cap, LANES):
        at = (lax.broadcasted_iota(jnp.int32, (count, LANES), 1) + start).astype(jnp.float32)
        pieces.append(jnp.sum(jnp.where(dest_col == at, id_col, 0.0), axis=0, keepdims=True))
    ids_at = jnp.concatenate(pieces, axis=1)
    block_ids = ids_at[:, :slots]
    slot_lane = lax.broadcasted_iota(jnp.int32, (1, slots), 1)
    last = functools.reduce(jnp.logical_or, [slot_lane == k * block + block - 1 for k in range(peers)])
    code = code_of(leader, bad).astype(jnp.float32)
    block_ids = jnp.where(last, code, block_ids)
    hdr = pad_lanes(block_ids, width)
    lead_hdr = jnp.broadcast_to(pad_lanes(ids_at[:, slots:], width), (SUB, width)).astype(jnp.bfloat16)
    even[cap : cap + SUB, :] = lead_hdr
    odd[cap : cap + SUB, :] = lead_hdr
    at = lax.broadcasted_iota(jnp.int32, (slots + cap, count), 0)
    pick[...] = jnp.where(at == dest, 1.0, 0.0).astype(jnp.bfloat16)

    for i in range(CHUNKS):
        copies[i].wait()
        rows = slice(i * chunk, (i + 1) * chunk)
        emb = emb_ref[rows, :]
        squares = jnp.sum(emb * emb, axis=1, keepdims=True)
        unit_ref[rows, :] = (emb * lax.rsqrt(squares + 1e-06)).astype(jnp.bfloat16)

    places = [(mine, 0), (even, cap + SUB), *[(ref, 0) for ref in far], (odd, cap + SUB), (mine_across, 0)]
    places += [(across, s * block) for s in range(reach - 1)]
    is_hdr = lax.broadcasted_iota(jnp.int32, (block, 1), 0) == block - 1
    tile = 256
    for start in range(0, width, tile):
        cols = slice(start, start + tile)
        acc = jnp.dot(pick[...], unit_ref[:, cols], preferred_element_type=jnp.float32)
        for k, (ref, at) in enumerate(places):
            rows = acc[k * block : (k + 1) * block]
            ref[at : at + block, cols] = jnp.where(is_hdr, hdr[:, cols], rows).astype(jnp.bfloat16)
        even[:cap, cols] = acc[slots:].astype(jnp.bfloat16)
        odd[:cap, cols] = acc[slots:].astype(jnp.bfloat16)


def relay_kernel(peers, block, lead_rows, even, odd, mine_across, across, lead_even, odd_out, ends, queries, *far):
    reach = peers // 2
    last = (reach - 2) * block
    odd_out[:lead_rows, :] = lead_even[:lead_rows, :]
    odd_out[lead_rows:, :] = across[last:, :]
    ends[:block, :] = odd[lead_rows:, :]
    ends[block:, :] = across[last:, :]
    for s in range(2, reach - 1):
        far[s - 2][...] = across[(s - 1) * block : s * block, :]
    queries[:lead_rows, :] = even[:lead_rows, :]
    queries[lead_rows : 2 * lead_rows, :] = lead_even[:lead_rows, :]
    queries[2 * lead_rows :, :] = mine_across[...]


def pass_kernel(block, lead_rows, even, lead_even, lead_odd, across, even_out, cols):
    even_out[:lead_rows, :] = lead_odd[:lead_rows, :]
    even_out[lead_rows:, :] = across[:block, :]
    for k, rows in enumerate((even, lead_even, lead_odd)):
        cols[k * lead_rows : (k + 1) * lead_rows, :] = rows[:lead_rows, :]


def collect_kernel(peers, block, lead_rows, me_ref, mine, even, odd, asked_y, even2, odd2, ends, *rest):
    reach = peers // 2
    far, far_across, own = rest[: reach - 3], rest[reach - 3 : 2 * reach - 6], rest[-1]
    rest = rest[2 * reach - 6 : -1]
    z = me_ref[0] // 2
    at_end = (z == 0) | (z == reach - 1)

    def put(k, src, start=0):
        own[k * block : (k + 1) * block, :] = src[start : start + block, :]

    def put_last(first, second, start, then):
        put(reach - 1, first, start)
        put(2 * reach - 1, second, then)

    put(0, mine)
    put(reach, asked_y, 2 * lead_rows)
    put(1, even, lead_rows)
    put(reach + 1, even2, lead_rows)
    for s in range(2, reach - 1):
        put(s, far[s - 2])
        put(reach + s, far_across[s - 2])
    pl.when(at_end)(functools.partial(put_last, ends, ends, 0, block))
    pl.when(jnp.logical_not(at_end))(functools.partial(put_last, odd, odd2, lead_rows, lead_rows))

    def keep(slot, src):
        at = peers * block + slot * lead_rows
        own[at : at + lead_rows, :] = src[:lead_rows, :]

    if reach == 4:
        pl.when(at_end)(functools.partial(keep, 0, even2))
        pl.when(jnp.logical_not(at_end))(functools.partial(keep, 0, odd2))
    else:
        for slot, src in enumerate(rest):
            keep(slot, src)


def lead_ids(rows, start, cap):
    return rows[start + cap : start + cap + SUB, :cap].astype(jnp.float32)[0:1]


def lead_column(rows, start, count, cap):
    gap = jnp.zeros((SUB, 1), jnp.float32)
    parts = []
    for k in range(count):
        parts += [as_column(lead_ids(rows, start + k * (cap + SUB), cap)), gap]
    return jnp.concatenate(parts, axis=0)


def lead_tops(columns, column_ids, queries, start, cap, diagonal):
    rows = queries[start : start + cap, :]
    scores = lax.dot_general(columns, rows, NT, preferred_element_type=jnp.float32)
    same = column_ids == lead_ids(queries, start, cap)
    if diagonal:
        r = lax.broadcasted_iota(jnp.int32, scores.shape, 0)
        l = lax.broadcasted_iota(jnp.int32, scores.shape, 1)
        same = same & (r != l)
    return jnp.max(jnp.where(same, scores, -1.0), axis=0, keepdims=True)


def lead_early_kernel(cap, asked, cols, cols_other, top):
    best = None
    for columns in (cols, cols_other):
        ids = lead_column(columns, 0, 3, cap)
        new = lead_tops(columns[...], ids, asked, 0, cap, columns is cols)
        best = new if best is None else jnp.maximum(best, new)
    top[...] = jnp.broadcast_to(best, top.shape)


def lead_late(rows, slots, cap, asked, asked_y):
    count = (rows.shape[0] - slots) // (cap + SUB)
    ids = lead_column(rows, slots, count, cap)
    places = ((asked, 0), (asked_y, 0), (asked, cap + SUB), (asked_y, cap + SUB))
    return [lead_tops(rows[slots:, :], ids, queries, start, cap, False) for queries, start in places]


def lead_best_kernel(slots, cap, early, asked, asked_y, near, near_other, own, top):
    best = lead_late(own, slots, cap, asked, asked_y)
    best[0] = jnp.maximum(best[0], early[0:1, :])
    for columns in (near, near_other):
        new = lead_tops(columns[...], lead_column(columns, 0, 3, cap), asked_y, 0, cap, False)
        best[1] = jnp.maximum(best[1], new)
    top[...] = jnp.concatenate(best + [jnp.full((4, cap), -1.0, jnp.float32)], axis=0)


def ids_of(rows, peers, block):
    width = rows.shape[1]
    lane = lax.broadcasted_iota(jnp.int32, (1, width), 1)
    total = jnp.zeros((1, width), jnp.float32)
    for k in range(peers):
        tail = rows[(k + 1) * block - SUB : (k + 1) * block, :].astype(jnp.float32)[SUB - 1 : SUB]
        total = jnp.where((lane >= k * block) & (lane < (k + 1) * block), tail, total)
    return total


def tops_of(rows, ids, queries, q_ids, diagonal, tile):
    slots = q_ids.shape[1]
    column = as_column(ids)[:slots]
    tops = []
    for start in range(0, slots, tile):
        stop = min(start + tile, slots)
        scores = lax.dot_general(rows[:slots, :], queries[start:stop, :], NT, preferred_element_type=jnp.float32)
        same = column == q_ids[:, start:stop]
        if diagonal:
            r = lax.broadcasted_iota(jnp.int32, scores.shape, 0)
            l = lax.broadcasted_iota(jnp.int32, scores.shape, 1) + start
            same = same & (r != l)
        tops.append(jnp.max(jnp.where(same, scores, -1.0), axis=0, keepdims=True))
    return jnp.concatenate(tops, axis=1)


def own_best_kernel(peers, block, own, top):
    slots = peers * block
    ids = ids_of(own, peers, block)
    top[0:1, :] = tops_of(own, ids, own, ids[:, :slots], True, 256)
    top[1:2, :] = ids[:, :slots]


def far_best_kernel(peers, block, edges, me_ref, own, far, top, asked, asked_y, lead_top, out, flag):
    width = own.shape[1]
    slots = peers * block
    own_ids, far_ids = top[1:2, :], ids_of(far, peers, block)
    lane = lax.broadcasted_iota(jnp.int32, (1, slots), 1)
    is_code = functools.reduce(jnp.logical_or, [lane == k * block + block - 1 for k in range(peers)])
    my_code = own_ids[:, block - 1 : block]
    odd = jnp.where(is_code & ((own_ids != my_code) | (far_ids[:, :slots] != my_code)), 1.0, 0.0)
    half = jnp.floor(my_code * 0.5)
    odd = jnp.maximum(jnp.max(odd, axis=1, keepdims=True), my_code - 2.0 * half)
    flag[...] = jnp.broadcast_to(odd, flag.shape)
    best = jnp.maximum(top[0:1, :], tops_of(far, far_ids, own, own_ids, False, 256))
    best = jnp.broadcast_to(pad_lanes(best, width), (8, width))
    reach = peers // 2
    pitch = -(-block // LANES) * LANES
    cap = out.shape[2] - pitch
    z, y = me_ref[0] // 2, me_ref[0] % 2
    none = jnp.full((1, cap), -1.0, jnp.float32)
    for k in range(peers):
        piece = best if k == 0 else pltpu.roll(best, width - k * block, 1)
        up = (z % 2 == 0) == (k % 2 == 1)
        row = z + jnp.where(up, k % reach, reach - k % reach)
        row = 2 * (row % reach) + (y if k < reach else 1 - y)
        out[row, :, :pitch] = piece[0:1, :pitch]
        out[k, :, pitch:] = none
    lead = [jnp.maximum(lead_top[i : i + 1, :], new) for i, new in enumerate(lead_late(far, slots, cap, asked, asked_y))]
    out[2 * z + y, :, pitch:] = lead[0]
    out[2 * z + 1 - y, :, pitch:] = lead[1]
    if edges:
        for at, to in ((1, 0), (reach - 2, reach - 1)):

            @pl.when(z == at)
            def _():
                out[2 * to + y, :, pitch:] = lead[2]
                out[2 * to + 1 - y, :, pitch:] = lead[3]


def final_kernel(peers, cap, info_ref, back_ref, out):
    count = info_ref.shape[1]
    pitch = back_ref.shape[2] - cap
    where = info_ref[1:2, :]
    rows = [back_ref[h] for h in range(peers)]
    lead = functools.reduce(jnp.maximum, [row[:, pitch:] for row in rows])
    total = jnp.zeros((1, count), jnp.float32)
    at = lax.broadcasted_iota(jnp.int32, (pitch, count), 0)
    cols = jnp.transpose(jnp.concatenate([row[:, :pitch] for row in rows], axis=0))
    for h in range(peers):
        hit = at + h * pitch == where
        total += jnp.sum(jnp.where(hit, cols[:, h : h + 1], 0.0), axis=0, keepdims=True)
    at = lax.broadcasted_iota(jnp.int32, (cap, count), 0) + peers * pitch
    total += jnp.sum(jnp.where(at == where, as_column(lead), 0.0), axis=0, keepdims=True)
    out[...] = total


def call(kernel, name, outs, in_specs, out_specs, scratch=(), flops=0, nbytes=0):
    return pl.pallas_call(
        kernel,
        name=name,
        out_shape=outs,
        in_specs=in_specs,
        out_specs=out_specs,
        scratch_shapes=list(scratch),
        compiler_params=pltpu.CompilerParams(vmem_limit_bytes=VMEM_LIMIT),
        cost_estimate=pl.CostEstimate(flops=flops, bytes_accessed=nbytes, transcendentals=0),
    )


def whole_exchange(embeddings, cluster_ids):
    count, width = embeddings.shape
    peers = lax.axis_size("dp")
    slots = 2 * count // peers
    squares = jnp.sum(embeddings * embeddings, axis=1, keepdims=True)
    unit = (embeddings * lax.rsqrt(squares + 1e-06)).astype(jnp.bfloat16)
    target = cluster_ids // CL_DEV
    onehot = (target[:, None] == jnp.arange(peers, dtype=jnp.int32)[None, :]).astype(jnp.int32)
    ranking = jnp.cumsum(onehot, axis=0) - 1
    position = jnp.sum(ranking * onehot, axis=1)
    where_to = target * slots + position
    total = peers * slots
    send_rows = jnp.zeros((total, width), jnp.bfloat16).at[where_to].set(unit)
    send_ids = jnp.full((total,), -1, jnp.int32).at[where_to].set(cluster_ids)
    own_rows = lax.all_to_all(send_rows, "dp", split_axis=0, concat_axis=0, tiled=True)
    own_ids = lax.all_to_all(send_ids, "dp", split_axis=0, concat_axis=0, tiled=True)
    swap = [(0, 1), (1, 0)]
    far_rows = lax.ppermute(own_rows, "owner", swap)
    far_ids = lax.ppermute(own_ids, "owner", swap)
    block = math.gcd(total, 512)
    column_pos = jnp.arange(total, dtype=jnp.int32)

    def block_best(start):
        queries = lax.dynamic_slice_in_dim(own_rows, start, block, 0)
        query_ids = lax.dynamic_slice_in_dim(own_ids, start, block, 0)
        row_pos = start + jnp.arange(block, dtype=jnp.int32)
        tops = []
        for rows, ids, own in ((own_rows, own_ids, True), (far_rows, far_ids, False)):
            scores = lax.dot_general(queries, rows, NT, preferred_element_type=jnp.float32)
            same = (query_ids[:, None] == ids[None, :]) & (ids[None, :] >= 0)
            if own:
                same = same & (row_pos[:, None] != column_pos[None, :])
            tops.append(jnp.max(jnp.where(same, scores, jnp.float32(-1.0)), axis=1))
        return jnp.maximum(tops[0], tops[1])

    starts = jnp.arange(total // block, dtype=jnp.int32) * block
    best = lax.map(block_best, starts).reshape(peers, slots)
    returned = lax.all_to_all(best, "dp", split_axis=0, concat_axis=0, tiled=True)
    return returned.reshape(-1)[where_to]


def local(embeddings, cluster_ids):
    count, width = embeddings.shape
    peers = lax.axis_size("dp")
    groups = lax.axis_size("groups")
    cap = 2 * count // peers
    mean = -(-(count - cap) // (peers - 1))
    block = -(-(mean + 1) // SUB) * SUB
    slots = peers * block
    pitch = -(-block // LANES) * LANES
    reach = peers // 2
    bf16, f32 = jnp.bfloat16, jnp.float32
    shape = jax.ShapeDtypeStruct
    me = lax.axis_index("dp")
    me1 = me.reshape(1)

    def dp_pairs(step):
        pairs = []
        for z in range(reach):
            for y in range(2):
                to = step(z, y)
                if to is not None:
                    pairs.append((2 * z + y, 2 * to[0] + to[1]))
        return pairs

    other_y = dp_pairs(lambda z, y: (z, 1 - y))
    up_pairs = dp_pairs(lambda z, y: (z + 1, y) if z + 1 < reach else None)
    down_pairs = dp_pairs(lambda z, y: (z - 1, y) if z > 0 else None)
    swap = [(0, 1), (1, 0)]

    ends_pairs = dp_pairs(lambda z, y: (reach - 1 - z, y) if z in (0, reach - 1) else None)
    shift_pairs = [
        dp_pairs(lambda z, y, s=s: ((z + (s if z % 2 == 0 else reach - s)) % reach, y)) for s in range(2, reach - 1)
    ]
    even_pairs = dp_pairs(lambda z, y: (z ^ 1, y))
    odd_pairs = dp_pairs(lambda z, y: (((z + 1) ^ 1) - 1, y) if 0 < z < reach - 1 else None)

    one = shape((block, width), bf16)
    lead_rows = cap + SUB
    message = shape((lead_rows + block, width), bf16)
    edges = reach == 4

    info, mine, mine_across, even, odd, across, *fars = call(
        functools.partial(pack_kernel, peers, cap, block),
        "pack",
        [shape((8, count), jnp.int32), one, one, message, message]
        + [shape(((reach - 1) * block, width), bf16)]
        + [one] * (reach - 3),
        [SMEM, VMEM, pl.BlockSpec(memory_space=pltpu.HBM)],
        [VMEM] * (3 + reach),
        [
            pltpu.VMEM((count, width), f32),
            pltpu.VMEM((count, width), bf16),
            pltpu.VMEM((slots + cap, count), bf16),
            pltpu.SemaphoreType.DMA((CHUNKS,)),
        ],
        flops=2 * (slots + cap) * count * width,
        nbytes=8 * count * width,
    )(me1, cluster_ids.reshape(1, count), embeddings)
    odd1 = lax.ppermute(odd, "dp", odd_pairs)
    even1 = lax.ppermute(even, "dp", even_pairs)
    across = lax.ppermute(across, "dp", other_y)
    fars = [lax.ppermute(rows, "dp", pairs) for rows, pairs in zip(fars, shift_pairs)]
    across, even1 = lax.optimization_barrier((across, even1))
    odd2, ends, asked, *fars_r = call(
        functools.partial(relay_kernel, peers, block, lead_rows),
        "relay",
        [message, shape((2 * block, width), bf16), shape((2 * lead_rows + block, width), bf16)] + [one] * (reach - 3),
        [VMEM] * 5,
        [VMEM] * reach,
        nbytes=2 * slots * width,
    )(even, odd, mine_across, across, even1)
    odd2 = lax.ppermute(odd2, "dp", odd_pairs)
    asked_y = lax.ppermute(asked, "dp", other_y)
    odd1, fars, ends, fars_r, across = lax.optimization_barrier((odd1, fars, ends, fars_r, across))
    even2, near_cols = call(
        functools.partial(pass_kernel, block, lead_rows),
        "pass_on",
        [message, shape((3 * lead_rows, width), bf16)],
        [VMEM] * 4,
        [VMEM] * 2,
        nbytes=8 * lead_rows * width,
    )(even, even1, odd1, across)
    even2 = lax.ppermute(even2, "dp", even_pairs)
    near_o = lax.ppermute(near_cols, "owner", swap)
    ends, fars_r, near_o = lax.optimization_barrier((ends, fars_r, near_o))
    ends = lax.ppermute(ends, "dp", ends_pairs)
    fars_r = [lax.ppermute(rows, "dp", pairs) for rows, pairs in zip(fars_r, shift_pairs)]
    early = call(
        functools.partial(lead_early_kernel, cap),
        "lead_early",
        shape((8, cap), f32),
        [VMEM] * 3,
        VMEM,
        flops=12 * cap * cap * width,
        nbytes=14 * cap * width,
    )(asked, near_cols, near_o)
    odd2, even2, ends, fars_r, asked_y, early = lax.optimization_barrier((odd2, even2, ends, fars_r, asked_y, early))
    late = []
    if not edges:
        is_even = (me // 2) % 2 == 0
        up = jnp.where(is_even, odd2[:lead_rows], even2[:lead_rows])
        down = jnp.where(is_even, even2[:lead_rows], odd2[:lead_rows])
        late = [up, down]
        for _ in range(reach - 3):
            up = lax.ppermute(up, "dp", up_pairs)
            down = lax.ppermute(down, "dp", down_pairs)
            late += [up, down]
    own = call(
        functools.partial(collect_kernel, peers, block, lead_rows),
        "collect",
        shape((slots + max(1, len(late)) * lead_rows, width), bf16),
        [SMEM] + [VMEM] * (7 + 2 * (reach - 3) + len(late)),
        VMEM,
        nbytes=4 * slots * width,
    )(me1, mine, even1, odd1, asked_y, even2, odd2, ends, *fars, *fars_r, *late)
    far = lax.ppermute(own, "owner", swap)
    lead_top = call(
        functools.partial(lead_best_kernel, slots, cap),
        "lead_best",
        shape((8, cap), f32),
        [VMEM] * 6,
        VMEM,
        flops=40 * cap * cap * width,
        nbytes=20 * cap * width,
    )(early, asked, asked_y, near_cols, near_o, own)
    top = call(
        functools.partial(own_best_kernel, peers, block),
        "own_best",
        shape((8, slots), f32),
        [VMEM],
        VMEM,
        flops=2 * slots * slots * width,
        nbytes=2 * slots * width,
    )(own)
    best, flag = call(
        functools.partial(far_best_kernel, peers, block, edges),
        "far_best",
        [shape((peers, 1, pitch + cap), f32), shape((8, LANES), f32)],
        [SMEM] + [VMEM] * 6,
        [VMEM] * 2,
        flops=2 * slots * slots * width,
        nbytes=4 * slots * width,
    )(me1, own, far, top, asked, asked_y, lead_top)
    back = lax.all_to_all(best, "dp", split_axis=0, concat_axis=0, tiled=True)
    flags = [flag]
    for k in range(1, groups):
        flags.append(lax.ppermute(flag, "groups", [(g, (g + k) % groups) for g in range(groups)]))
    odd = functools.reduce(jnp.maximum, flags)[0, 0]
    nearest = call(
        functools.partial(final_kernel, peers, cap),
        "final",
        shape((1, count), f32),
        [VMEM] * 2,
        VMEM,
        flops=0,
        nbytes=4 * count,
    )(info, back).reshape(count)
    return lax.cond(odd > 0, whole_exchange, lambda e, c: nearest, embeddings, cluster_ids)


def solution(mesh):
    return jax.shard_map(
        local,
        mesh=mesh,
        in_specs=(P(("groups", "dp", "owner"), None), P(("groups", "dp", "owner"))),
        out_specs=P(("groups", "dp", "owner")),
        check_vma=False,
    )
```

```python
import functools
import math

import jax
import jax.numpy as jnp
from jax import lax
from jax.experimental import pallas as pl
from jax.experimental.pallas import tpu as pltpu
from jax.sharding import PartitionSpec as P

CL_DEV = 8
LANES = 128
CHUNKS = 4
SUB = 16
VMEM_LIMIT = 14 * 1024 * 1024
VMEM = pl.BlockSpec(memory_space=pltpu.VMEM)
SMEM = pl.BlockSpec(memory_space=pltpu.SMEM)
NT = (((1,), (1,)), ((), ()))


def pad_lanes(row, width):
    extra = width - row.shape[1]
    if extra == 0:
        return row
    return jnp.concatenate([row, jnp.zeros((row.shape[0], extra), row.dtype)], axis=1)


def as_column(row):
    return jnp.transpose(jnp.broadcast_to(row, (8, row.shape[1])))[:, 0:1]


def code_of(leader, bad):
    return 16 + 2 * leader + bad


def pack_kernel(peers, cap, block, me_ref, ids_ref, emb_hbm, info_ref, mine, mine_across, even, odd, across, *rest):
    far, (emb_ref, unit_ref, pick, sem) = rest[:-4], rest[-4:]
    count, width = emb_ref.shape
    chunk = count // CHUNKS
    copies = []
    for i in range(CHUNKS):
        rows = pl.ds(i * chunk, chunk)
        copies.append(pltpu.make_async_copy(emb_hbm.at[rows, :], emb_ref.at[rows, :], sem.at[i]))
        copies[-1].start()
    ids = ids_ref[...]
    target = jnp.right_shift(ids, int(math.log2(CL_DEV)))
    local_id = jnp.bitwise_and(ids, CL_DEV - 1)
    tio = lax.broadcasted_iota(jnp.int32, (peers, 1), 0)
    onehot = (lax.broadcasted_iota(jnp.int32, (peers, count), 0) == target).astype(jnp.int32)
    lane = lax.broadcasted_iota(jnp.int32, (peers, count), 1)
    cum = onehot
    step = 1
    while step < count:
        cum = cum + jnp.where(lane >= step, pltpu.roll(cum, step, 1), 0)
        step *= 2
    rank = jnp.sum(cum * onehot, axis=0, keepdims=True) - 1
    counts = cum[:, count - 1 : count]
    leader = jnp.min(jnp.where(counts == cap, tio, peers - 1), axis=0, keepdims=True)
    others = jnp.max(jnp.where(tio == leader, cap - counts, counts), axis=0, keepdims=True)
    lead_short = jnp.max(jnp.where(tio == leader, cap - counts, 0), axis=0, keepdims=True)
    bad = ((others > block - 1) | (lead_short != 0)).astype(jnp.int32)
    is_lead = target == leader
    slots = peers * block
    fits = rank < block - 1
    reach = peers // 2
    z = me_ref[0] // 2
    shift = jnp.right_shift(target, 1) - z
    shift = jnp.where(z % 2 == 0, shift, -shift)
    shift = jnp.where(shift < 0, shift + reach, shift)
    place = jnp.where(jnp.bitwise_and(target, 1) == me_ref[0] % 2, shift, reach + shift)
    dest = jnp.where(is_lead, slots + rank, jnp.where(fits, place * block + rank, -1))
    pitch = -(-block // LANES) * LANES
    final = jnp.where(is_lead, peers * pitch + rank, target * pitch + rank)
    row8 = lax.broadcasted_iota(jnp.int32, (8, count), 0)
    info_ref[...] = jnp.where(row8 == 0, dest, final)

    both = jnp.where(row8 == 0, dest, local_id + 1).astype(jnp.float32)
    both = jnp.transpose(both)
    dest_col, id_col = both[:, 0:1], both[:, 1:2]
    pieces = []
    for start in range(0, slots + cap, LANES):
        at = (lax.broadcasted_iota(jnp.int32, (count, LANES), 1) + start).astype(jnp.float32)
        pieces.append(jnp.sum(jnp.where(dest_col == at, id_col, 0.0), axis=0, keepdims=True))
    ids_at = jnp.concatenate(pieces, axis=1)
    block_ids = ids_at[:, :slots]
    slot_lane = lax.broadcasted_iota(jnp.int32, (1, slots), 1)
    last = functools.reduce(jnp.logical_or, [slot_lane == k * block + block - 1 for k in range(peers)])
    code = code_of(leader, bad).astype(jnp.float32)
    block_ids = jnp.where(last, code, block_ids)
    hdr = pad_lanes(block_ids, width)
    lead_hdr = jnp.broadcast_to(pad_lanes(ids_at[:, slots:], width), (SUB, width)).astype(jnp.bfloat16)
    even[cap : cap + SUB, :] = lead_hdr
    odd[cap : cap + SUB, :] = lead_hdr
    at = lax.broadcasted_iota(jnp.int32, (slots + cap, count), 0)
    pick[...] = jnp.where(at == dest, 1.0, 0.0).astype(jnp.bfloat16)

    for i in range(CHUNKS):
        copies[i].wait()
        rows = slice(i * chunk, (i + 1) * chunk)
        emb = emb_ref[rows, :]
        squares = jnp.sum(emb * emb, axis=1, keepdims=True)
        unit_ref[rows, :] = (emb * lax.rsqrt(squares + 1e-06)).astype(jnp.bfloat16)

    places = [(mine, 0), (even, cap + SUB), *[(ref, 0) for ref in far], (odd, cap + SUB), (mine_across, 0)]
    places += [(across, s * block) for s in range(reach - 1)]
    is_hdr = lax.broadcasted_iota(jnp.int32, (block, 1), 0) == block - 1
    tile = 256
    for start in range(0, width, tile):
        cols = slice(start, start + tile)
        acc = jnp.dot(pick[...], unit_ref[:, cols], preferred_element_type=jnp.float32)
        for k, (ref, at) in enumerate(places):
            rows = acc[k * block : (k + 1) * block]
            ref[at : at + block, cols] = jnp.where(is_hdr, hdr[:, cols], rows).astype(jnp.bfloat16)
        even[:cap, cols] = acc[slots:].astype(jnp.bfloat16)
        odd[:cap, cols] = acc[slots:].astype(jnp.bfloat16)


def relay_kernel(peers, block, lead_rows, even, odd, mine_across, across, lead_even, odd_out, ends, queries, cols, *far):
    reach = peers // 2
    last = (reach - 2) * block
    odd_out[:lead_rows, :] = lead_even[:lead_rows, :]
    odd_out[lead_rows:, :] = across[last:, :]
    cols[:lead_rows, :] = even[:lead_rows, :]
    cols[lead_rows:, :] = lead_even[:lead_rows, :]
    ends[:block, :] = odd[lead_rows:, :]
    ends[block:, :] = across[last:, :]
    for s in range(2, reach - 1):
        far[s - 2][...] = across[(s - 1) * block : s * block, :]
    queries[:lead_rows, :] = even[:lead_rows, :]
    queries[lead_rows : 2 * lead_rows, :] = lead_even[:lead_rows, :]
    queries[2 * lead_rows :, :] = mine_across[...]


def pass_kernel(block, lead_rows, lead_odd, across, even_out):
    even_out[:lead_rows, :] = lead_odd[:lead_rows, :]
    even_out[lead_rows:, :] = across[:block, :]


def collect_kernel(peers, block, lead_rows, me_ref, mine, even, odd, asked_y, even2, odd2, ends, *rest):
    reach = peers // 2
    far, far_across, own = rest[: reach - 3], rest[reach - 3 : 2 * reach - 6], rest[-1]
    rest = rest[2 * reach - 6 : -1]
    z = me_ref[0] // 2
    at_end = (z == 0) | (z == reach - 1)

    def put(k, src, start=0):
        own[k * block : (k + 1) * block, :] = src[start : start + block, :]

    def put_last(first, second, start, then):
        put(reach - 1, first, start)
        put(2 * reach - 1, second, then)

    put(0, mine)
    put(reach, asked_y, 2 * lead_rows)
    put(1, even, lead_rows)
    put(reach + 1, even2, lead_rows)
    for s in range(2, reach - 1):
        put(s, far[s - 2])
        put(reach + s, far_across[s - 2])
    pl.when(at_end)(functools.partial(put_last, ends, ends, 0, block))
    pl.when(jnp.logical_not(at_end))(functools.partial(put_last, odd, odd2, lead_rows, lead_rows))

    def keep(slot, src):
        at = peers * block + slot * lead_rows
        own[at : at + lead_rows, :] = src[:lead_rows, :]

    keep((own.shape[0] - peers * block) // lead_rows - 1, odd)
    if reach == 4:
        pl.when(at_end)(functools.partial(keep, 0, even2))
        pl.when(jnp.logical_not(at_end))(functools.partial(keep, 0, odd2))
    else:
        for slot, src in enumerate(rest):
            keep(slot, src)


def lead_ids(rows, start, cap):
    return rows[start + cap : start + cap + SUB, :cap].astype(jnp.float32)[0:1]


def lead_column(rows, start, count, cap):
    gap = jnp.zeros((SUB, 1), jnp.float32)
    parts = []
    for k in range(count):
        parts += [as_column(lead_ids(rows, start + k * (cap + SUB), cap)), gap]
    return jnp.concatenate(parts, axis=0)


def lead_tops(columns, column_ids, queries, start, cap, diagonal):
    rows = queries[start : start + cap, :]
    scores = lax.dot_general(columns, rows, NT, preferred_element_type=jnp.float32)
    same = column_ids == lead_ids(queries, start, cap)
    if diagonal:
        r = lax.broadcasted_iota(jnp.int32, scores.shape, 0)
        l = lax.broadcasted_iota(jnp.int32, scores.shape, 1)
        same = same & (r != l)
    return jnp.max(jnp.where(same, scores, -1.0), axis=0, keepdims=True)


def lead_early_kernel(cap, asked, asked_y, cols, cols_other, top):
    best = [jnp.full((1, cap), -1.0, jnp.float32)] * 8
    for columns in (cols, cols_other):
        ids = lead_column(columns, 0, 2, cap)
        for i, queries in enumerate((asked, asked_y)):
            new = lead_tops(columns[...], ids, queries, 0, cap, i == 0 and columns is cols)
            best[i] = jnp.maximum(best[i], new)
    top[...] = jnp.concatenate(best, axis=0)


def lead_late(rows, slots, cap, asked, asked_y):
    count = (rows.shape[0] - slots) // (cap + SUB)
    ids = lead_column(rows, slots, count, cap)
    places = ((asked, 0), (asked_y, 0), (asked, cap + SUB), (asked_y, cap + SUB))
    return [lead_tops(rows[slots:, :], ids, queries, start, cap, False) for queries, start in places]


def lead_best_kernel(slots, cap, early, asked, asked_y, own, top):
    late = lead_late(own, slots, cap, asked, asked_y)
    best = [jnp.maximum(early[i : i + 1, :], new) for i, new in enumerate(late)]
    top[...] = jnp.concatenate(best + [jnp.full((4, cap), -1.0, jnp.float32)], axis=0)


def ids_of(rows, peers, block):
    width = rows.shape[1]
    lane = lax.broadcasted_iota(jnp.int32, (1, width), 1)
    total = jnp.zeros((1, width), jnp.float32)
    for k in range(peers):
        tail = rows[(k + 1) * block - SUB : (k + 1) * block, :].astype(jnp.float32)[SUB - 1 : SUB]
        total = jnp.where((lane >= k * block) & (lane < (k + 1) * block), tail, total)
    return total


def tops_of(rows, ids, queries, q_ids, diagonal, tile):
    slots = q_ids.shape[1]
    column = as_column(ids)[:slots]
    tops = []
    for start in range(0, slots, tile):
        stop = min(start + tile, slots)
        scores = lax.dot_general(rows[:slots, :], queries[start:stop, :], NT, preferred_element_type=jnp.float32)
        same = column == q_ids[:, start:stop]
        if diagonal:
            r = lax.broadcasted_iota(jnp.int32, scores.shape, 0)
            l = lax.broadcasted_iota(jnp.int32, scores.shape, 1) + start
            same = same & (r != l)
        tops.append(jnp.max(jnp.where(same, scores, -1.0), axis=0, keepdims=True))
    return jnp.concatenate(tops, axis=1)


def own_best_kernel(peers, block, own, top):
    slots = peers * block
    ids = ids_of(own, peers, block)
    top[0:1, :] = tops_of(own, ids, own, ids[:, :slots], True, 256)
    top[1:2, :] = ids[:, :slots]


def far_best_kernel(peers, block, edges, me_ref, own, far, top, asked, asked_y, lead_top, out, flag):
    width = own.shape[1]
    slots = peers * block
    own_ids, far_ids = top[1:2, :], ids_of(far, peers, block)
    lane = lax.broadcasted_iota(jnp.int32, (1, slots), 1)
    is_code = functools.reduce(jnp.logical_or, [lane == k * block + block - 1 for k in range(peers)])
    my_code = own_ids[:, block - 1 : block]
    odd = jnp.where(is_code & ((own_ids != my_code) | (far_ids[:, :slots] != my_code)), 1.0, 0.0)
    half = jnp.floor(my_code * 0.5)
    odd = jnp.maximum(jnp.max(odd, axis=1, keepdims=True), my_code - 2.0 * half)
    flag[...] = jnp.broadcast_to(odd, flag.shape)
    best = jnp.maximum(top[0:1, :], tops_of(far, far_ids, own, own_ids, False, 256))
    best = jnp.broadcast_to(pad_lanes(best, width), (8, width))
    reach = peers // 2
    pitch = -(-block // LANES) * LANES
    cap = out.shape[2] - pitch
    z, y = me_ref[0] // 2, me_ref[0] % 2
    none = jnp.full((1, cap), -1.0, jnp.float32)
    for k in range(peers):
        piece = best if k == 0 else pltpu.roll(best, width - k * block, 1)
        up = (z % 2 == 0) == (k % 2 == 1)
        row = z + jnp.where(up, k % reach, reach - k % reach)
        row = 2 * (row % reach) + (y if k < reach else 1 - y)
        out[row, :, :pitch] = piece[0:1, :pitch]
        out[k, :, pitch:] = none
    lead = [jnp.maximum(lead_top[i : i + 1, :], new) for i, new in enumerate(lead_late(far, slots, cap, asked, asked_y))]
    out[2 * z + y, :, pitch:] = lead[0]
    out[2 * z + 1 - y, :, pitch:] = lead[1]
    if edges:
        for at, to in ((1, 0), (reach - 2, reach - 1)):

            @pl.when(z == at)
            def _():
                out[2 * to + y, :, pitch:] = lead[2]
                out[2 * to + 1 - y, :, pitch:] = lead[3]


def final_kernel(peers, cap, info_ref, back_ref, out):
    count = info_ref.shape[1]
    pitch = back_ref.shape[2] - cap
    where = info_ref[1:2, :]
    rows = [back_ref[h] for h in range(peers)]
    lead = functools.reduce(jnp.maximum, [row[:, pitch:] for row in rows])
    total = jnp.zeros((1, count), jnp.float32)
    at = lax.broadcasted_iota(jnp.int32, (pitch, count), 0)
    cols = jnp.transpose(jnp.concatenate([row[:, :pitch] for row in rows], axis=0))
    for h in range(peers):
        hit = at + h * pitch == where
        total += jnp.sum(jnp.where(hit, cols[:, h : h + 1], 0.0), axis=0, keepdims=True)
    at = lax.broadcasted_iota(jnp.int32, (cap, count), 0) + peers * pitch
    total += jnp.sum(jnp.where(at == where, as_column(lead), 0.0), axis=0, keepdims=True)
    out[...] = total


def call(kernel, name, outs, in_specs, out_specs, scratch=(), flops=0, nbytes=0):
    return pl.pallas_call(
        kernel,
        name=name,
        out_shape=outs,
        in_specs=in_specs,
        out_specs=out_specs,
        scratch_shapes=list(scratch),
        compiler_params=pltpu.CompilerParams(vmem_limit_bytes=VMEM_LIMIT),
        cost_estimate=pl.CostEstimate(flops=flops, bytes_accessed=nbytes, transcendentals=0),
    )


def whole_exchange(embeddings, cluster_ids):
    count, width = embeddings.shape
    peers = lax.axis_size("dp")
    slots = 2 * count // peers
    squares = jnp.sum(embeddings * embeddings, axis=1, keepdims=True)
    unit = (embeddings * lax.rsqrt(squares + 1e-06)).astype(jnp.bfloat16)
    target = cluster_ids // CL_DEV
    onehot = (target[:, None] == jnp.arange(peers, dtype=jnp.int32)[None, :]).astype(jnp.int32)
    ranking = jnp.cumsum(onehot, axis=0) - 1
    position = jnp.sum(ranking * onehot, axis=1)
    where_to = target * slots + position
    total = peers * slots
    send_rows = jnp.zeros((total, width), jnp.bfloat16).at[where_to].set(unit)
    send_ids = jnp.full((total,), -1, jnp.int32).at[where_to].set(cluster_ids)
    own_rows = lax.all_to_all(send_rows, "dp", split_axis=0, concat_axis=0, tiled=True)
    own_ids = lax.all_to_all(send_ids, "dp", split_axis=0, concat_axis=0, tiled=True)
    swap = [(0, 1), (1, 0)]
    far_rows = lax.ppermute(own_rows, "owner", swap)
    far_ids = lax.ppermute(own_ids, "owner", swap)
    block = math.gcd(total, 512)
    column_pos = jnp.arange(total, dtype=jnp.int32)

    def block_best(start):
        queries = lax.dynamic_slice_in_dim(own_rows, start, block, 0)
        query_ids = lax.dynamic_slice_in_dim(own_ids, start, block, 0)
        row_pos = start + jnp.arange(block, dtype=jnp.int32)
        tops = []
        for rows, ids, own in ((own_rows, own_ids, True), (far_rows, far_ids, False)):
            scores = lax.dot_general(queries, rows, NT, preferred_element_type=jnp.float32)
            same = (query_ids[:, None] == ids[None, :]) & (ids[None, :] >= 0)
            if own:
                same = same & (row_pos[:, None] != column_pos[None, :])
            tops.append(jnp.max(jnp.where(same, scores, jnp.float32(-1.0)), axis=1))
        return jnp.maximum(tops[0], tops[1])

    starts = jnp.arange(total // block, dtype=jnp.int32) * block
    best = lax.map(block_best, starts).reshape(peers, slots)
    returned = lax.all_to_all(best, "dp", split_axis=0, concat_axis=0, tiled=True)
    return returned.reshape(-1)[where_to]


def local(embeddings, cluster_ids):
    count, width = embeddings.shape
    peers = lax.axis_size("dp")
    groups = lax.axis_size("groups")
    cap = 2 * count // peers
    mean = -(-(count - cap) // (peers - 1))
    block = -(-(mean + 1) // SUB) * SUB
    slots = peers * block
    pitch = -(-block // LANES) * LANES
    reach = peers // 2
    bf16, f32 = jnp.bfloat16, jnp.float32
    shape = jax.ShapeDtypeStruct
    me = lax.axis_index("dp")
    me1 = me.reshape(1)

    def dp_pairs(step):
        pairs = []
        for z in range(reach):
            for y in range(2):
                to = step(z, y)
                if to is not None:
                    pairs.append((2 * z + y, 2 * to[0] + to[1]))
        return pairs

    other_y = dp_pairs(lambda z, y: (z, 1 - y))
    up_pairs = dp_pairs(lambda z, y: (z + 1, y) if z + 1 < reach else None)
    down_pairs = dp_pairs(lambda z, y: (z - 1, y) if z > 0 else None)
    swap = [(0, 1), (1, 0)]

    ends_pairs = dp_pairs(lambda z, y: (reach - 1 - z, y) if z in (0, reach - 1) else None)
    shift_pairs = [
        dp_pairs(lambda z, y, s=s: ((z + (s if z % 2 == 0 else reach - s)) % reach, y)) for s in range(2, reach - 1)
    ]
    even_pairs = dp_pairs(lambda z, y: (z ^ 1, y))
    odd_pairs = dp_pairs(lambda z, y: (((z + 1) ^ 1) - 1, y) if 0 < z < reach - 1 else None)

    one = shape((block, width), bf16)
    lead_rows = cap + SUB
    message = shape((lead_rows + block, width), bf16)
    edges = reach == 4

    info, mine, mine_across, even, odd, across, *fars = call(
        functools.partial(pack_kernel, peers, cap, block),
        "pack",
        [shape((8, count), jnp.int32), one, one, message, message]
        + [shape(((reach - 1) * block, width), bf16)]
        + [one] * (reach - 3),
        [SMEM, VMEM, pl.BlockSpec(memory_space=pltpu.HBM)],
        [VMEM] * (3 + reach),
        [
            pltpu.VMEM((count, width), f32),
            pltpu.VMEM((count, width), bf16),
            pltpu.VMEM((slots + cap, count), bf16),
            pltpu.SemaphoreType.DMA((CHUNKS,)),
        ],
        flops=2 * (slots + cap) * count * width,
        nbytes=8 * count * width,
    )(me1, cluster_ids.reshape(1, count), embeddings)
    odd1 = lax.ppermute(odd, "dp", odd_pairs)
    even1 = lax.ppermute(even, "dp", even_pairs)
    across = lax.ppermute(across, "dp", other_y)
    fars = [lax.ppermute(rows, "dp", pairs) for rows, pairs in zip(fars, shift_pairs)]
    across, even1, fars = lax.optimization_barrier((across, even1, fars))
    odd2, ends, asked, near_cols, *fars_r = call(
        functools.partial(relay_kernel, peers, block, lead_rows),
        "relay",
        [
            message,
            shape((2 * block, width), bf16),
            shape((2 * lead_rows + block, width), bf16),
            shape((2 * lead_rows, width), bf16),
        ]
        + [one] * (reach - 3),
        [VMEM] * 5,
        [VMEM] * (1 + reach),
        nbytes=2 * slots * width,
    )(even, odd, mine_across, across, even1)
    odd2 = lax.ppermute(odd2, "dp", odd_pairs)
    asked_y = lax.ppermute(asked, "dp", other_y)
    near_o = lax.ppermute(near_cols, "owner", swap)
    even2 = call(
        functools.partial(pass_kernel, block, lead_rows),
        "pass_on",
        message,
        [VMEM] * 2,
        VMEM,
        nbytes=8 * lead_rows * width,
    )(odd1, across)
    even2 = lax.ppermute(even2, "dp", even_pairs)
    ends = lax.ppermute(ends, "dp", ends_pairs)
    fars_r = [lax.ppermute(rows, "dp", pairs) for rows, pairs in zip(fars_r, shift_pairs)]
    odd2, asked_y, near_cols, near_o = lax.optimization_barrier((odd2, asked_y, near_cols, near_o))
    early = call(
        functools.partial(lead_early_kernel, cap),
        "lead_early",
        shape((8, cap), f32),
        [VMEM] * 4,
        VMEM,
        flops=24 * cap * cap * width,
        nbytes=14 * cap * width,
    )(asked, asked_y, near_cols, near_o)
    odd2, even2, ends, fars_r, asked_y, early = lax.optimization_barrier((odd2, even2, ends, fars_r, asked_y, early))
    late = []
    if not edges:
        is_even = (me // 2) % 2 == 0
        up = jnp.where(is_even, odd2[:lead_rows], even2[:lead_rows])
        down = jnp.where(is_even, even2[:lead_rows], odd2[:lead_rows])
        late = [up, down]
        for _ in range(reach - 3):
            up = lax.ppermute(up, "dp", up_pairs)
            down = lax.ppermute(down, "dp", down_pairs)
            late += [up, down]
    own = call(
        functools.partial(collect_kernel, peers, block, lead_rows),
        "collect",
        shape((slots + (1 + max(1, len(late))) * lead_rows, width), bf16),
        [SMEM] + [VMEM] * (7 + 2 * (reach - 3) + len(late)),
        VMEM,
        nbytes=4 * slots * width,
    )(me1, mine, even1, odd1, asked_y, even2, odd2, ends, *fars, *fars_r, *late)
    far = lax.ppermute(own, "owner", swap)
    lead_top = call(
        functools.partial(lead_best_kernel, slots, cap),
        "lead_best",
        shape((8, cap), f32),
        [VMEM] * 4,
        VMEM,
        flops=40 * cap * cap * width,
        nbytes=20 * cap * width,
    )(early, asked, asked_y, own)
    top = call(
        functools.partial(own_best_kernel, peers, block),
        "own_best",
        shape((8, slots), f32),
        [VMEM],
        VMEM,
        flops=2 * slots * slots * width,
        nbytes=2 * slots * width,
    )(own)
    best, flag = call(
        functools.partial(far_best_kernel, peers, block, edges),
        "far_best",
        [shape((peers, 1, pitch + cap), f32), shape((8, LANES), f32)],
        [SMEM] + [VMEM] * 6,
        [VMEM] * 2,
        flops=2 * slots * slots * width,
        nbytes=4 * slots * width,
    )(me1, own, far, top, asked, asked_y, lead_top)
    back = lax.all_to_all(best, "dp", split_axis=0, concat_axis=0, tiled=True)
    flags = [flag]
    for k in range(1, groups):
        flags.append(lax.ppermute(flag, "groups", [(g, (g + k) % groups) for g in range(groups)]))
    odd = functools.reduce(jnp.maximum, flags)[0, 0]
    nearest = call(
        functools.partial(final_kernel, peers, cap),
        "final",
        shape((1, count), f32),
        [VMEM] * 2,
        VMEM,
        flops=0,
        nbytes=4 * count,
    )(info, back).reshape(count)
    return lax.cond(odd > 0, whole_exchange, lambda e, c: nearest, embeddings, cluster_ids)


def solution(mesh):
    return jax.shard_map(
        local,
        mesh=mesh,
        in_specs=(P(("groups", "dp", "owner"), None), P(("groups", "dp", "owner"))),
        out_specs=P(("groups", "dp", "owner")),
        check_vma=False,
    )
```

```python
import functools
import math

import jax
import jax.numpy as jnp
from jax import lax
from jax.experimental import pallas as pl
from jax.experimental.pallas import tpu as pltpu
from jax.sharding import PartitionSpec as P

CL_DEV = 8
LANES = 128
CHUNKS = 4
FIRST = 2
SUB = 16
VMEM_LIMIT = 14 * 1024 * 1024
VMEM = pl.BlockSpec(memory_space=pltpu.VMEM)
SMEM = pl.BlockSpec(memory_space=pltpu.SMEM)
NT = (((1,), (1,)), ((), ()))


def pad_lanes(row, width):
    extra = width - row.shape[1]
    if extra == 0:
        return row
    return jnp.concatenate([row, jnp.zeros((row.shape[0], extra), row.dtype)], axis=1)


def as_column(row):
    return jnp.transpose(jnp.broadcast_to(row, (8, row.shape[1])))[:, 0:1]


def code_of(leader, bad):
    return 16 + 2 * leader + bad


def pack_kernel(peers, cap, block, me_ref, ids_ref, emb_hbm, info_ref, mine, mine_across, even, odd, across, *rest):
    far, (emb_ref, unit_ref, pick, sem) = rest[:-4], rest[-4:]
    count, width = emb_ref.shape
    chunk = count // CHUNKS
    copies = []
    for i in range(CHUNKS):
        rows = pl.ds(i * chunk, chunk)
        copies.append(pltpu.make_async_copy(emb_hbm.at[rows, :], emb_ref.at[rows, :], sem.at[i]))
        copies[-1].start()
    ids = ids_ref[...]
    target = jnp.right_shift(ids, int(math.log2(CL_DEV)))
    local_id = jnp.bitwise_and(ids, CL_DEV - 1)
    tio = lax.broadcasted_iota(jnp.int32, (peers, 1), 0)
    onehot = (lax.broadcasted_iota(jnp.int32, (peers, count), 0) == target).astype(jnp.int32)
    lane = lax.broadcasted_iota(jnp.int32, (peers, count), 1)
    cum = onehot
    step = 1
    while step < count:
        cum = cum + jnp.where(lane >= step, pltpu.roll(cum, step, 1), 0)
        step *= 2
    rank = jnp.sum(cum * onehot, axis=0, keepdims=True) - 1
    counts = cum[:, count - 1 : count]
    leader = jnp.min(jnp.where(counts == cap, tio, peers - 1), axis=0, keepdims=True)
    others = jnp.max(jnp.where(tio == leader, cap - counts, counts), axis=0, keepdims=True)
    lead_short = jnp.max(jnp.where(tio == leader, cap - counts, 0), axis=0, keepdims=True)
    bad = ((others > block - 1) | (lead_short != 0)).astype(jnp.int32)
    is_lead = target == leader
    slots = peers * block
    fits = rank < block - 1
    reach = peers // 2
    z = me_ref[0] // 2
    shift = jnp.right_shift(target, 1) - z
    shift = jnp.where(z % 2 == 0, shift, -shift)
    shift = jnp.where(shift < 0, shift + reach, shift)
    place = jnp.where(jnp.bitwise_and(target, 1) == me_ref[0] % 2, shift, reach + shift)
    dest = jnp.where(is_lead, slots + rank, jnp.where(fits, place * block + rank, -1))
    pitch = -(-block // LANES) * LANES
    final = jnp.where(is_lead, peers * pitch + rank, target * pitch + rank)
    row8 = lax.broadcasted_iota(jnp.int32, (8, count), 0)
    info_ref[...] = jnp.where(row8 == 0, dest, final)

    both = jnp.where(row8 == 0, dest, local_id + 1).astype(jnp.float32)
    both = jnp.transpose(both)
    dest_col, id_col = both[:, 0:1], both[:, 1:2]
    pieces = []
    for start in range(0, slots + cap, LANES):
        at = (lax.broadcasted_iota(jnp.int32, (count, LANES), 1) + start).astype(jnp.float32)
        pieces.append(jnp.sum(jnp.where(dest_col == at, id_col, 0.0), axis=0, keepdims=True))
    ids_at = jnp.concatenate(pieces, axis=1)
    block_ids = ids_at[:, :slots]
    slot_lane = lax.broadcasted_iota(jnp.int32, (1, slots), 1)
    last = functools.reduce(jnp.logical_or, [slot_lane == k * block + block - 1 for k in range(peers)])
    code = code_of(leader, bad).astype(jnp.float32)
    block_ids = jnp.where(last, code, block_ids)
    hdr = pad_lanes(block_ids, width)
    lead_hdr = jnp.broadcast_to(pad_lanes(ids_at[:, slots:], width), (SUB, width)).astype(jnp.bfloat16)
    even[cap : cap + SUB, :] = lead_hdr
    odd[cap : cap + SUB, :] = lead_hdr
    at = lax.broadcasted_iota(jnp.int32, (slots + cap, count), 0)
    pick[...] = jnp.where(at == dest, 1.0, 0.0).astype(jnp.bfloat16)

    for i in range(CHUNKS):
        copies[i].wait()
        rows = slice(i * chunk, (i + 1) * chunk)
        emb = emb_ref[rows, :]
        squares = jnp.sum(emb * emb, axis=1, keepdims=True)
        unit_ref[rows, :] = (emb * lax.rsqrt(squares + 1e-06)).astype(jnp.bfloat16)

    places = [(mine, 0), (even, cap + SUB), *[(ref, 0) for ref in far], (odd, cap + SUB), (mine_across, 0)]
    places += [(across, s * block) for s in range(reach - 1)]
    is_hdr = lax.broadcasted_iota(jnp.int32, (block, 1), 0) == block - 1
    tile = 256
    for start in range(0, width, tile):
        cols = slice(start, start + tile)
        acc = jnp.dot(pick[...], unit_ref[:, cols], preferred_element_type=jnp.float32)
        for k, (ref, at) in enumerate(places):
            rows = acc[k * block : (k + 1) * block]
            ref[at : at + block, cols] = jnp.where(is_hdr, hdr[:, cols], rows).astype(jnp.bfloat16)
        even[:cap, cols] = acc[slots:].astype(jnp.bfloat16)
        odd[:cap, cols] = acc[slots:].astype(jnp.bfloat16)


def relay_kernel(peers, block, lead_rows, even, odd, mine_across, across, lead_even, odd_out, ends, queries, cols, *far):
    reach = peers // 2
    last = (reach - 2) * block
    odd_out[:lead_rows, :] = lead_even[:lead_rows, :]
    odd_out[lead_rows:, :] = across[last:, :]
    cols[:lead_rows, :] = even[:lead_rows, :]
    cols[lead_rows:, :] = lead_even[:lead_rows, :]
    ends[:block, :] = odd[lead_rows:, :]
    ends[block:, :] = across[last:, :]
    for s in range(2, reach - 1):
        far[s - 2][...] = across[(s - 1) * block : s * block, :]
    queries[:lead_rows, :] = even[:lead_rows, :]
    queries[lead_rows : 2 * lead_rows, :] = lead_even[:lead_rows, :]
    queries[2 * lead_rows :, :] = mine_across[...]


def pass_kernel(block, lead_rows, lead_odd, across, even_out):
    even_out[:lead_rows, :] = lead_odd[:lead_rows, :]
    even_out[lead_rows:, :] = across[:block, :]


def collect_kernel(peers, block, lead_rows, me_ref, mine, even, odd, asked_y, even2, odd2, ends, *rest):
    reach = peers // 2
    far, far_across, own = rest[: reach - 3], rest[reach - 3 : 2 * reach - 6], rest[-3]
    first, second = rest[-2:]
    rest = rest[2 * reach - 6 : -3]
    z = me_ref[0] // 2
    at_end = (z == 0) | (z == reach - 1)

    def put(k, src, start=0):
        own[k * block : (k + 1) * block, :] = src[start : start + block, :]
        there, at = (first, k) if k < FIRST else (second, k - FIRST)
        there[at * block : (at + 1) * block, :] = src[start : start + block, :]

    def put_last(first, second, start, then):
        put(reach - 1, first, start)
        put(2 * reach - 1, second, then)

    put(0, mine)
    put(reach, asked_y, 2 * lead_rows)
    put(1, even, lead_rows)
    put(reach + 1, even2, lead_rows)
    for s in range(2, reach - 1):
        put(s, far[s - 2])
        put(reach + s, far_across[s - 2])
    pl.when(at_end)(functools.partial(put_last, ends, ends, 0, block))
    pl.when(jnp.logical_not(at_end))(functools.partial(put_last, odd, odd2, lead_rows, lead_rows))

    def keep(slot, src):
        at = FIRST * block + slot * lead_rows
        first[at : at + lead_rows, :] = src[:lead_rows, :]

    keep((first.shape[0] - FIRST * block) // lead_rows - 1, odd)
    if reach == 4:
        pl.when(at_end)(functools.partial(keep, 0, even2))
        pl.when(jnp.logical_not(at_end))(functools.partial(keep, 0, odd2))
    else:
        for slot, src in enumerate(rest):
            keep(slot, src)


def lead_ids(rows, start, cap):
    return rows[start + cap : start + cap + SUB, :cap].astype(jnp.float32)[0:1]


def lead_column(rows, start, count, cap):
    gap = jnp.zeros((SUB, 1), jnp.float32)
    parts = []
    for k in range(count):
        parts += [as_column(lead_ids(rows, start + k * (cap + SUB), cap)), gap]
    return jnp.concatenate(parts, axis=0)


def lead_tops(columns, column_ids, queries, start, cap, diagonal):
    rows = queries[start : start + cap, :]
    scores = lax.dot_general(columns, rows, NT, preferred_element_type=jnp.float32)
    same = column_ids == lead_ids(queries, start, cap)
    if diagonal:
        r = lax.broadcasted_iota(jnp.int32, scores.shape, 0)
        l = lax.broadcasted_iota(jnp.int32, scores.shape, 1)
        same = same & (r != l)
    return jnp.max(jnp.where(same, scores, -1.0), axis=0, keepdims=True)


def lead_early_kernel(cap, asked, asked_y, cols, cols_other, top):
    best = [jnp.full((1, cap), -1.0, jnp.float32)] * 8
    for columns in (cols, cols_other):
        ids = lead_column(columns, 0, 2, cap)
        for i, queries in enumerate((asked, asked_y)):
            new = lead_tops(columns[...], ids, queries, 0, cap, i == 0 and columns is cols)
            best[i] = jnp.maximum(best[i], new)
    top[...] = jnp.concatenate(best, axis=0)


def lead_late(rows, start, cap, asked, asked_y):
    lead_rows = cap + SUB
    count = (rows.shape[0] - start) // lead_rows
    ids = lead_column(rows, start, count, cap)
    best = [lead_tops(rows[start:, :], ids, queries, 0, cap, False) for queries in (asked, asked_y)]
    stop = (count - 1) * lead_rows
    for queries in (asked, asked_y):
        best.append(lead_tops(rows[start : start + stop, :], ids[:stop], queries, lead_rows, cap, False))
    return best


def lead_best_kernel(cap, block, early, asked, asked_y, first, top):
    late = lead_late(first, FIRST * block, cap, asked, asked_y)
    best = [jnp.maximum(early[i : i + 1, :], new) for i, new in enumerate(late)]
    top[...] = jnp.concatenate(best + [jnp.full((4, cap), -1.0, jnp.float32)], axis=0)


def ids_of(rows, blocks, block):
    width = rows.shape[1]
    lane = lax.broadcasted_iota(jnp.int32, (1, width), 1)
    total = jnp.zeros((1, width), jnp.float32)
    for i, k in enumerate(blocks):
        tail = rows[(i + 1) * block - SUB : (i + 1) * block, :].astype(jnp.float32)[SUB - 1 : SUB]
        total = jnp.where((lane >= k * block) & (lane < (k + 1) * block), tail, total)
    return total


def tops_of(rows, ids, begin, queries, q_ids, diagonal, tile):
    slots = q_ids.shape[1]
    column = as_column(ids)[begin : begin + rows.shape[0]]
    tops = []
    for start in range(0, slots, tile):
        stop = min(start + tile, slots)
        scores = lax.dot_general(rows, queries[start:stop, :], NT, preferred_element_type=jnp.float32)
        same = column == q_ids[:, start:stop]
        if diagonal:
            r = lax.broadcasted_iota(jnp.int32, scores.shape, 0)
            l = lax.broadcasted_iota(jnp.int32, scores.shape, 1) + start
            same = same & (r != l)
        tops.append(jnp.max(jnp.where(same, scores, -1.0), axis=0, keepdims=True))
    return jnp.concatenate(tops, axis=1)


def own_best_kernel(peers, block, own, top):
    slots = peers * block
    ids = ids_of(own, range(peers), block)
    top[0:1, :] = tops_of(own[...], ids, 0, own, ids[:, :slots], True, 256)
    top[1:2, :] = ids[:, :slots]


def first_best_kernel(peers, block, cap, own, first, top, asked, asked_y, lead_top, out, lead_out):
    slots = peers * block
    ids = ids_of(first, range(FIRST), block)
    best = tops_of(first[: FIRST * block, :], ids, 0, own, top[1:2, :], False, 256)
    out[0:1, :] = jnp.maximum(top[0:1, :], best)
    out[1:2, :] = top[1:2, :]
    out[2:3, :] = ids[:, :slots]
    late = lead_late(first, FIRST * block, cap, asked, asked_y)
    best = [jnp.maximum(lead_top[i : i + 1, :], new) for i, new in enumerate(late)]
    lead_out[...] = jnp.concatenate(best + [jnp.full((4, cap), -1.0, jnp.float32)], axis=0)


def far_best_kernel(peers, block, edges, me_ref, own, second, top, lead_top, out, flag):
    width = own.shape[1]
    slots = peers * block
    own_ids = top[1:2, :]
    second_ids = ids_of(second, range(FIRST, peers), block)
    lane = lax.broadcasted_iota(jnp.int32, (1, slots), 1)
    far_ids = jnp.where(lane < FIRST * block, top[2:3, :], second_ids[:, :slots])
    is_code = functools.reduce(jnp.logical_or, [lane == k * block + block - 1 for k in range(peers)])
    my_code = own_ids[:, block - 1 : block]
    odd = jnp.where(is_code & ((own_ids != my_code) | (far_ids != my_code)), 1.0, 0.0)
    half = jnp.floor(my_code * 0.5)
    odd = jnp.maximum(jnp.max(odd, axis=1, keepdims=True), my_code - 2.0 * half)
    flag[...] = jnp.broadcast_to(odd, flag.shape)
    best = tops_of(second[...], second_ids, FIRST * block, own, own_ids, False, 256)
    best = jnp.maximum(top[0:1, :], best)
    best = jnp.broadcast_to(pad_lanes(best, width), (8, width))
    reach = peers // 2
    pitch = -(-block // LANES) * LANES
    cap = out.shape[2] - pitch
    z, y = me_ref[0] // 2, me_ref[0] % 2
    none = jnp.full((1, cap), -1.0, jnp.float32)
    for k in range(peers):
        piece = best if k == 0 else pltpu.roll(best, width - k * block, 1)
        up = (z % 2 == 0) == (k % 2 == 1)
        row = z + jnp.where(up, k % reach, reach - k % reach)
        row = 2 * (row % reach) + (y if k < reach else 1 - y)
        out[row, :, :pitch] = piece[0:1, :pitch]
        out[k, :, pitch:] = none
    lead = [lead_top[i : i + 1, :] for i in range(4)]
    out[2 * z + y, :, pitch:] = lead[0]
    out[2 * z + 1 - y, :, pitch:] = lead[1]
    if edges:
        for at, to in ((1, 0), (reach - 2, reach - 1)):

            @pl.when(z == at)
            def _():
                out[2 * to + y, :, pitch:] = lead[2]
                out[2 * to + 1 - y, :, pitch:] = lead[3]


def final_kernel(peers, cap, info_ref, back_ref, out):
    count = info_ref.shape[1]
    pitch = back_ref.shape[2] - cap
    where = info_ref[1:2, :]
    rows = [back_ref[h] for h in range(peers)]
    lead = functools.reduce(jnp.maximum, [row[:, pitch:] for row in rows])
    total = jnp.zeros((1, count), jnp.float32)
    at = lax.broadcasted_iota(jnp.int32, (pitch, count), 0)
    cols = jnp.transpose(jnp.concatenate([row[:, :pitch] for row in rows], axis=0))
    for h in range(peers):
        hit = at + h * pitch == where
        total += jnp.sum(jnp.where(hit, cols[:, h : h + 1], 0.0), axis=0, keepdims=True)
    at = lax.broadcasted_iota(jnp.int32, (cap, count), 0) + peers * pitch
    total += jnp.sum(jnp.where(at == where, as_column(lead), 0.0), axis=0, keepdims=True)
    out[...] = total


def call(kernel, name, outs, in_specs, out_specs, scratch=(), flops=0, nbytes=0):
    return pl.pallas_call(
        kernel,
        name=name,
        out_shape=outs,
        in_specs=in_specs,
        out_specs=out_specs,
        scratch_shapes=list(scratch),
        compiler_params=pltpu.CompilerParams(vmem_limit_bytes=VMEM_LIMIT),
        cost_estimate=pl.CostEstimate(flops=flops, bytes_accessed=nbytes, transcendentals=0),
    )


def whole_exchange(embeddings, cluster_ids):
    count, width = embeddings.shape
    peers = lax.axis_size("dp")
    slots = 2 * count // peers
    squares = jnp.sum(embeddings * embeddings, axis=1, keepdims=True)
    unit = (embeddings * lax.rsqrt(squares + 1e-06)).astype(jnp.bfloat16)
    target = cluster_ids // CL_DEV
    onehot = (target[:, None] == jnp.arange(peers, dtype=jnp.int32)[None, :]).astype(jnp.int32)
    ranking = jnp.cumsum(onehot, axis=0) - 1
    position = jnp.sum(ranking * onehot, axis=1)
    where_to = target * slots + position
    total = peers * slots
    send_rows = jnp.zeros((total, width), jnp.bfloat16).at[where_to].set(unit)
    send_ids = jnp.full((total,), -1, jnp.int32).at[where_to].set(cluster_ids)
    own_rows = lax.all_to_all(send_rows, "dp", split_axis=0, concat_axis=0, tiled=True)
    own_ids = lax.all_to_all(send_ids, "dp", split_axis=0, concat_axis=0, tiled=True)
    swap = [(0, 1), (1, 0)]
    far_rows = lax.ppermute(own_rows, "owner", swap)
    far_ids = lax.ppermute(own_ids, "owner", swap)
    block = math.gcd(total, 512)
    column_pos = jnp.arange(total, dtype=jnp.int32)

    def block_best(start):
        queries = lax.dynamic_slice_in_dim(own_rows, start, block, 0)
        query_ids = lax.dynamic_slice_in_dim(own_ids, start, block, 0)
        row_pos = start + jnp.arange(block, dtype=jnp.int32)
        tops = []
        for rows, ids, own in ((own_rows, own_ids, True), (far_rows, far_ids, False)):
            scores = lax.dot_general(queries, rows, NT, preferred_element_type=jnp.float32)
            same = (query_ids[:, None] == ids[None, :]) & (ids[None, :] >= 0)
            if own:
                same = same & (row_pos[:, None] != column_pos[None, :])
            tops.append(jnp.max(jnp.where(same, scores, jnp.float32(-1.0)), axis=1))
        return jnp.maximum(tops[0], tops[1])

    starts = jnp.arange(total // block, dtype=jnp.int32) * block
    best = lax.map(block_best, starts).reshape(peers, slots)
    returned = lax.all_to_all(best, "dp", split_axis=0, concat_axis=0, tiled=True)
    return returned.reshape(-1)[where_to]


def local(embeddings, cluster_ids):
    count, width = embeddings.shape
    peers = lax.axis_size("dp")
    groups = lax.axis_size("groups")
    cap = 2 * count // peers
    mean = -(-(count - cap) // (peers - 1))
    block = -(-(mean + 1) // SUB) * SUB
    slots = peers * block
    pitch = -(-block // LANES) * LANES
    reach = peers // 2
    bf16, f32 = jnp.bfloat16, jnp.float32
    shape = jax.ShapeDtypeStruct
    me = lax.axis_index("dp")
    me1 = me.reshape(1)

    def dp_pairs(step):
        pairs = []
        for z in range(reach):
            for y in range(2):
                to = step(z, y)
                if to is not None:
                    pairs.append((2 * z + y, 2 * to[0] + to[1]))
        return pairs

    other_y = dp_pairs(lambda z, y: (z, 1 - y))
    up_pairs = dp_pairs(lambda z, y: (z + 1, y) if z + 1 < reach else None)
    down_pairs = dp_pairs(lambda z, y: (z - 1, y) if z > 0 else None)
    swap = [(0, 1), (1, 0)]

    ends_pairs = dp_pairs(lambda z, y: (reach - 1 - z, y) if z in (0, reach - 1) else None)
    shift_pairs = [
        dp_pairs(lambda z, y, s=s: ((z + (s if z % 2 == 0 else reach - s)) % reach, y)) for s in range(2, reach - 1)
    ]
    even_pairs = dp_pairs(lambda z, y: (z ^ 1, y))
    odd_pairs = dp_pairs(lambda z, y: (((z + 1) ^ 1) - 1, y) if 0 < z < reach - 1 else None)

    one = shape((block, width), bf16)
    lead_rows = cap + SUB
    message = shape((lead_rows + block, width), bf16)
    edges = reach == 4

    info, mine, mine_across, even, odd, across, *fars = call(
        functools.partial(pack_kernel, peers, cap, block),
        "pack",
        [shape((8, count), jnp.int32), one, one, message, message]
        + [shape(((reach - 1) * block, width), bf16)]
        + [one] * (reach - 3),
        [SMEM, VMEM, pl.BlockSpec(memory_space=pltpu.HBM)],
        [VMEM] * (3 + reach),
        [
            pltpu.VMEM((count, width), f32),
            pltpu.VMEM((count, width), bf16),
            pltpu.VMEM((slots + cap, count), bf16),
            pltpu.SemaphoreType.DMA((CHUNKS,)),
        ],
        flops=2 * (slots + cap) * count * width,
        nbytes=8 * count * width,
    )(me1, cluster_ids.reshape(1, count), embeddings)
    odd1 = lax.ppermute(odd, "dp", odd_pairs)
    even1 = lax.ppermute(even, "dp", even_pairs)
    across = lax.ppermute(across, "dp", other_y)
    fars = [lax.ppermute(rows, "dp", pairs) for rows, pairs in zip(fars, shift_pairs)]
    across, even1, fars = lax.optimization_barrier((across, even1, fars))
    odd2, ends, asked, near_cols, *fars_r = call(
        functools.partial(relay_kernel, peers, block, lead_rows),
        "relay",
        [
            message,
            shape((2 * block, width), bf16),
            shape((2 * lead_rows + block, width), bf16),
            shape((2 * lead_rows, width), bf16),
        ]
        + [one] * (reach - 3),
        [VMEM] * 5,
        [VMEM] * (1 + reach),
        nbytes=2 * slots * width,
    )(even, odd, mine_across, across, even1)
    odd2 = lax.ppermute(odd2, "dp", odd_pairs)
    asked_y = lax.ppermute(asked, "dp", other_y)
    near_o = lax.ppermute(near_cols, "owner", swap)
    even2 = call(
        functools.partial(pass_kernel, block, lead_rows),
        "pass_on",
        message,
        [VMEM] * 2,
        VMEM,
        nbytes=8 * lead_rows * width,
    )(odd1, across)
    even2 = lax.ppermute(even2, "dp", even_pairs)
    ends = lax.ppermute(ends, "dp", ends_pairs)
    fars_r = [lax.ppermute(rows, "dp", pairs) for rows, pairs in zip(fars_r, shift_pairs)]
    odd2, asked_y, near_cols, near_o = lax.optimization_barrier((odd2, asked_y, near_cols, near_o))
    early = call(
        functools.partial(lead_early_kernel, cap),
        "lead_early",
        shape((8, cap), f32),
        [VMEM] * 4,
        VMEM,
        flops=24 * cap * cap * width,
        nbytes=14 * cap * width,
    )(asked, asked_y, near_cols, near_o)
    odd2, even2, ends, fars_r, asked_y, early = lax.optimization_barrier((odd2, even2, ends, fars_r, asked_y, early))
    late = []
    if not edges:
        is_even = (me // 2) % 2 == 0
        up = jnp.where(is_even, odd2[:lead_rows], even2[:lead_rows])
        down = jnp.where(is_even, even2[:lead_rows], odd2[:lead_rows])
        late = [up, down]
        for _ in range(reach - 3):
            up = lax.ppermute(up, "dp", up_pairs)
            down = lax.ppermute(down, "dp", down_pairs)
            late += [up, down]
    own, first, second = call(
        functools.partial(collect_kernel, peers, block, lead_rows),
        "collect",
        [
            shape((slots, width), bf16),
            shape((FIRST * block + (1 + max(1, len(late))) * lead_rows, width), bf16),
            shape((slots - FIRST * block, width), bf16),
        ],
        [SMEM] + [VMEM] * (7 + 2 * (reach - 3) + len(late)),
        [VMEM] * 3,
        nbytes=4 * slots * width,
    )(me1, mine, even1, odd1, asked_y, even2, odd2, ends, *fars, *fars_r, *late)
    first_o = lax.ppermute(first, "owner", swap)
    second_o = lax.ppermute(second, "owner", swap)
    lead_top = call(
        functools.partial(lead_best_kernel, cap, block),
        "lead_best",
        shape((8, cap), f32),
        [VMEM] * 4,
        VMEM,
        flops=40 * cap * cap * width,
        nbytes=20 * cap * width,
    )(early, asked, asked_y, first)
    top = call(
        functools.partial(own_best_kernel, peers, block),
        "own_best",
        shape((8, slots), f32),
        [VMEM],
        VMEM,
        flops=2 * slots * slots * width,
        nbytes=2 * slots * width,
    )(own)
    top, lead_top = call(
        functools.partial(first_best_kernel, peers, block, cap),
        "first_best",
        [shape((8, slots), f32), shape((8, cap), f32)],
        [VMEM] * 6,
        [VMEM] * 2,
        flops=2 * FIRST * block * slots * width + 14 * cap * cap * width,
        nbytes=4 * slots * width,
    )(own, first_o, top, asked, asked_y, lead_top)
    best, flag = call(
        functools.partial(far_best_kernel, peers, block, edges),
        "far_best",
        [shape((peers, 1, pitch + cap), f32), shape((8, LANES), f32)],
        [SMEM] + [VMEM] * 4,
        [VMEM] * 2,
        flops=2 * slots * slots * width,
        nbytes=4 * slots * width,
    )(me1, own, second_o, top, lead_top)
    back = lax.all_to_all(best, "dp", split_axis=0, concat_axis=0, tiled=True)
    flags = [flag]
    for k in range(1, groups):
        flags.append(lax.ppermute(flag, "groups", [(g, (g + k) % groups) for g in range(groups)]))
    odd = functools.reduce(jnp.maximum, flags)[0, 0]
    nearest = call(
        functools.partial(final_kernel, peers, cap),
        "final",
        shape((1, count), f32),
        [VMEM] * 2,
        VMEM,
        flops=0,
        nbytes=4 * count,
    )(info, back).reshape(count)
    return lax.cond(odd > 0, whole_exchange, lambda e, c: nearest, embeddings, cluster_ids)


def solution(mesh):
    return jax.shard_map(
        local,
        mesh=mesh,
        in_specs=(P(("groups", "dp", "owner"), None), P(("groups", "dp", "owner"))),
        out_specs=P(("groups", "dp", "owner")),
        check_vma=False,
    )
```

```python
import functools
import math

import jax
import jax.numpy as jnp
from jax import lax
from jax.experimental import pallas as pl
from jax.experimental.pallas import tpu as pltpu
from jax.sharding import PartitionSpec as P

CL_DEV = 8
LANES = 128
CHUNKS = 4
FIRST = 2
SUB = 16
VMEM_LIMIT = 14 * 1024 * 1024
VMEM = pl.BlockSpec(memory_space=pltpu.VMEM)
SMEM = pl.BlockSpec(memory_space=pltpu.SMEM)
NT = (((1,), (1,)), ((), ()))


def pad_lanes(row, width):
    extra = width - row.shape[1]
    if extra == 0:
        return row
    return jnp.concatenate([row, jnp.zeros((row.shape[0], extra), row.dtype)], axis=1)


def as_column(row):
    return jnp.transpose(jnp.broadcast_to(row, (8, row.shape[1])))[:, 0:1]


def code_of(leader, bad):
    return 16 + 2 * leader + bad


def pack_kernel(peers, cap, block, me_ref, ids_ref, emb_hbm, info_ref, mine, mine_across, even, odd, across, *rest):
    far, (emb_ref, unit_ref, pick, sem) = rest[:-4], rest[-4:]
    count, width = emb_ref.shape
    chunk = count // CHUNKS
    copies = []
    for i in range(CHUNKS):
        rows = pl.ds(i * chunk, chunk)
        copies.append(pltpu.make_async_copy(emb_hbm.at[rows, :], emb_ref.at[rows, :], sem.at[i]))
        copies[-1].start()
    ids = ids_ref[...]
    target = jnp.right_shift(ids, int(math.log2(CL_DEV)))
    local_id = jnp.bitwise_and(ids, CL_DEV - 1)
    tio = lax.broadcasted_iota(jnp.int32, (peers, 1), 0)
    onehot = (lax.broadcasted_iota(jnp.int32, (peers, count), 0) == target).astype(jnp.int32)
    lane = lax.broadcasted_iota(jnp.int32, (peers, count), 1)
    cum = onehot
    step = 1
    while step < count:
        cum = cum + jnp.where(lane >= step, pltpu.roll(cum, step, 1), 0)
        step *= 2
    rank = jnp.sum(cum * onehot, axis=0, keepdims=True) - 1
    counts = cum[:, count - 1 : count]
    leader = jnp.min(jnp.where(counts == cap, tio, peers - 1), axis=0, keepdims=True)
    others = jnp.max(jnp.where(tio == leader, cap - counts, counts), axis=0, keepdims=True)
    lead_short = jnp.max(jnp.where(tio == leader, cap - counts, 0), axis=0, keepdims=True)
    bad = ((others > block - 1) | (lead_short != 0)).astype(jnp.int32)
    is_lead = target == leader
    slots = peers * block
    fits = rank < block - 1
    reach = peers // 2
    z = me_ref[0] // 2
    shift = jnp.right_shift(target, 1) - z
    shift = jnp.where(z % 2 == 0, shift, -shift)
    shift = jnp.where(shift < 0, shift + reach, shift)
    place = jnp.where(jnp.bitwise_and(target, 1) == me_ref[0] % 2, shift, reach + shift)
    dest = jnp.where(is_lead, slots + rank, jnp.where(fits, place * block + rank, -1))
    pitch = -(-block // LANES) * LANES
    final = jnp.where(is_lead, peers * pitch + rank, target * pitch + rank)
    row8 = lax.broadcasted_iota(jnp.int32, (8, count), 0)
    info_ref[...] = jnp.where(row8 == 0, dest, final)

    both = jnp.where(row8 == 0, dest, local_id + 1).astype(jnp.float32)
    both = jnp.transpose(both)
    dest_col, id_col = both[:, 0:1], both[:, 1:2]
    pieces = []
    for start in range(0, slots + cap, LANES):
        at = (lax.broadcasted_iota(jnp.int32, (count, LANES), 1) + start).astype(jnp.float32)
        pieces.append(jnp.sum(jnp.where(dest_col == at, id_col, 0.0), axis=0, keepdims=True))
    ids_at = jnp.concatenate(pieces, axis=1)
    block_ids = ids_at[:, :slots]
    slot_lane = lax.broadcasted_iota(jnp.int32, (1, slots), 1)
    last = functools.reduce(jnp.logical_or, [slot_lane == k * block + block - 1 for k in range(peers)])
    code = code_of(leader, bad).astype(jnp.float32)
    block_ids = jnp.where(last, code, block_ids)
    hdr = pad_lanes(block_ids, width)
    lead_hdr = jnp.broadcast_to(pad_lanes(ids_at[:, slots:], width), (SUB, width)).astype(jnp.bfloat16)
    even[cap : cap + SUB, :] = lead_hdr
    odd[cap : cap + SUB, :] = lead_hdr
    at = lax.broadcasted_iota(jnp.int32, (slots + cap, count), 0)
    pick[...] = jnp.where(at == dest, 1.0, 0.0).astype(jnp.bfloat16)

    for i in range(CHUNKS):
        copies[i].wait()
        rows = slice(i * chunk, (i + 1) * chunk)
        emb = emb_ref[rows, :]
        squares = jnp.sum(emb * emb, axis=1, keepdims=True)
        unit_ref[rows, :] = (emb * lax.rsqrt(squares + 1e-06)).astype(jnp.bfloat16)

    places = [(mine, 0), (even, cap + SUB), *[(ref, 0) for ref in far], (odd, cap + SUB), (mine_across, 0)]
    places += [(across, s * block) for s in range(reach - 1)]
    is_hdr = lax.broadcasted_iota(jnp.int32, (block, 1), 0) == block - 1
    tile = 512
    for start in range(0, width, tile):
        cols = slice(start, start + tile)
        acc = jnp.dot(pick[...], unit_ref[:, cols], preferred_element_type=jnp.float32)
        for k, (ref, at) in enumerate(places):
            rows = acc[k * block : (k + 1) * block]
            ref[at : at + block, cols] = jnp.where(is_hdr, hdr[:, cols], rows).astype(jnp.bfloat16)
        even[:cap, cols] = acc[slots:].astype(jnp.bfloat16)
        odd[:cap, cols] = acc[slots:].astype(jnp.bfloat16)


def relay_kernel(peers, block, lead_rows, even, odd, mine_across, across, lead_even, odd_out, ends, queries, cols, *far):
    reach = peers // 2
    last = (reach - 2) * block
    odd_out[:lead_rows, :] = lead_even[:lead_rows, :]
    odd_out[lead_rows:, :] = across[last:, :]
    cols[:lead_rows, :] = even[:lead_rows, :]
    cols[lead_rows:, :] = lead_even[:lead_rows, :]
    ends[:block, :] = odd[lead_rows:, :]
    ends[block:, :] = across[last:, :]
    for s in range(2, reach - 1):
        far[s - 2][...] = across[(s - 1) * block : s * block, :]
    queries[:lead_rows, :] = even[:lead_rows, :]
    queries[lead_rows : 2 * lead_rows, :] = lead_even[:lead_rows, :]
    queries[2 * lead_rows :, :] = mine_across[...]


def pass_kernel(block, lead_rows, lead_odd, across, even_out):
    even_out[:lead_rows, :] = lead_odd[:lead_rows, :]
    even_out[lead_rows:, :] = across[:block, :]


def collect_kernel(peers, block, lead_rows, me_ref, mine, even, odd, asked_y, even2, odd2, ends, *rest):
    reach = peers // 2
    far, far_across, own = rest[: reach - 3], rest[reach - 3 : 2 * reach - 6], rest[-3]
    first, second = rest[-2:]
    rest = rest[2 * reach - 6 : -3]
    z = me_ref[0] // 2
    at_end = (z == 0) | (z == reach - 1)

    def put(k, src, start=0):
        own[k * block : (k + 1) * block, :] = src[start : start + block, :]
        there, at = (first, k) if k < FIRST else (second, k - FIRST)
        there[at * block : (at + 1) * block, :] = src[start : start + block, :]

    def put_last(first, second, start, then):
        put(reach - 1, first, start)
        put(2 * reach - 1, second, then)

    put(0, mine)
    put(reach, asked_y, 2 * lead_rows)
    put(1, even, lead_rows)
    put(reach + 1, even2, lead_rows)
    for s in range(2, reach - 1):
        put(s, far[s - 2])
        put(reach + s, far_across[s - 2])
    pl.when(at_end)(functools.partial(put_last, ends, ends, 0, block))
    pl.when(jnp.logical_not(at_end))(functools.partial(put_last, odd, odd2, lead_rows, lead_rows))

    def keep(slot, src):
        at = FIRST * block + slot * lead_rows
        first[at : at + lead_rows, :] = src[:lead_rows, :]

    keep((first.shape[0] - FIRST * block) // lead_rows - 1, odd)
    if reach == 4:
        pl.when(at_end)(functools.partial(keep, 0, even2))
        pl.when(jnp.logical_not(at_end))(functools.partial(keep, 0, odd2))
    else:
        for slot, src in enumerate(rest):
            keep(slot, src)


def lead_ids(rows, start, cap):
    return rows[start + cap : start + cap + SUB, :cap].astype(jnp.float32)[0:1]


def lead_column(rows, start, count, cap):
    gap = jnp.zeros((SUB, 1), jnp.float32)
    parts = []
    for k in range(count):
        parts += [as_column(lead_ids(rows, start + k * (cap + SUB), cap)), gap]
    return jnp.concatenate(parts, axis=0)


def lead_tops(columns, column_ids, queries, start, cap, diagonal):
    rows = queries[start : start + cap, :]
    scores = lax.dot_general(columns, rows, NT, preferred_element_type=jnp.float32)
    same = column_ids == lead_ids(queries, start, cap)
    if diagonal:
        r = lax.broadcasted_iota(jnp.int32, scores.shape, 0)
        l = lax.broadcasted_iota(jnp.int32, scores.shape, 1)
        same = same & (r != l)
    return jnp.max(jnp.where(same, scores, -1.0), axis=0, keepdims=True)


def lead_early_kernel(cap, asked, asked_y, cols, cols_other, top):
    best = [jnp.full((1, cap), -1.0, jnp.float32)] * 8
    for columns in (cols, cols_other):
        ids = lead_column(columns, 0, 2, cap)
        for i, queries in enumerate((asked, asked_y)):
            new = lead_tops(columns[...], ids, queries, 0, cap, i == 0 and columns is cols)
            best[i] = jnp.maximum(best[i], new)
    top[...] = jnp.concatenate(best, axis=0)


def lead_late(rows, start, cap, asked, asked_y):
    lead_rows = cap + SUB
    count = (rows.shape[0] - start) // lead_rows
    ids = lead_column(rows, start, count, cap)
    best = [lead_tops(rows[start:, :], ids, queries, 0, cap, False) for queries in (asked, asked_y)]
    stop = (count - 1) * lead_rows
    for queries in (asked, asked_y):
        best.append(lead_tops(rows[start : start + stop, :], ids[:stop], queries, lead_rows, cap, False))
    return best


def lead_best_kernel(cap, block, early, asked, asked_y, first, top):
    late = lead_late(first, FIRST * block, cap, asked, asked_y)
    best = [jnp.maximum(early[i : i + 1, :], new) for i, new in enumerate(late)]
    top[...] = jnp.concatenate(best + [jnp.full((4, cap), -1.0, jnp.float32)], axis=0)


def ids_of(rows, blocks, block):
    width = rows.shape[1]
    lane = lax.broadcasted_iota(jnp.int32, (1, width), 1)
    total = jnp.zeros((1, width), jnp.float32)
    for i, k in enumerate(blocks):
        tail = rows[(i + 1) * block - SUB : (i + 1) * block, :].astype(jnp.float32)[SUB - 1 : SUB]
        total = jnp.where((lane >= k * block) & (lane < (k + 1) * block), tail, total)
    return total


def tops_of(rows, ids, begin, queries, q_ids, diagonal, tile):
    slots = q_ids.shape[1]
    column = as_column(ids)[begin : begin + rows.shape[0]]
    tops = []
    for start in range(0, slots, tile):
        stop = min(start + tile, slots)
        scores = lax.dot_general(rows, queries[start:stop, :], NT, preferred_element_type=jnp.float32)
        same = column == q_ids[:, start:stop]
        if diagonal:
            r = lax.broadcasted_iota(jnp.int32, scores.shape, 0)
            l = lax.broadcasted_iota(jnp.int32, scores.shape, 1) + start
            same = same & (r != l)
        tops.append(jnp.max(jnp.where(same, scores, -1.0), axis=0, keepdims=True))
    return jnp.concatenate(tops, axis=1)


def own_best_kernel(peers, block, own, top):
    slots = peers * block
    ids = ids_of(own, range(peers), block)
    top[0:1, :] = tops_of(own[...], ids, 0, own, ids[:, :slots], True, 1024)
    top[1:2, :] = ids[:, :slots]


def first_best_kernel(peers, block, cap, own, first, top, asked, asked_y, lead_top, out, lead_out):
    slots = peers * block
    ids = ids_of(first, range(FIRST), block)
    best = tops_of(first[: FIRST * block, :], ids, 0, own, top[1:2, :], False, 1024)
    out[0:1, :] = jnp.maximum(top[0:1, :], best)
    out[1:2, :] = top[1:2, :]
    out[2:3, :] = ids[:, :slots]
    late = lead_late(first, FIRST * block, cap, asked, asked_y)
    best = [jnp.maximum(lead_top[i : i + 1, :], new) for i, new in enumerate(late)]
    lead_out[...] = jnp.concatenate(best + [jnp.full((4, cap), -1.0, jnp.float32)], axis=0)


def far_best_kernel(peers, block, edges, me_ref, own, second, top, lead_top, out, flag):
    width = own.shape[1]
    slots = peers * block
    own_ids = top[1:2, :]
    second_ids = ids_of(second, range(FIRST, peers), block)
    lane = lax.broadcasted_iota(jnp.int32, (1, slots), 1)
    far_ids = jnp.where(lane < FIRST * block, top[2:3, :], second_ids[:, :slots])
    is_code = functools.reduce(jnp.logical_or, [lane == k * block + block - 1 for k in range(peers)])
    my_code = own_ids[:, block - 1 : block]
    odd = jnp.where(is_code & ((own_ids != my_code) | (far_ids != my_code)), 1.0, 0.0)
    half = jnp.floor(my_code * 0.5)
    odd = jnp.maximum(jnp.max(odd, axis=1, keepdims=True), my_code - 2.0 * half)
    flag[...] = jnp.broadcast_to(odd, flag.shape)
    best = tops_of(second[...], second_ids, FIRST * block, own, own_ids, False, 1024)
    best = jnp.maximum(top[0:1, :], best)
    best = jnp.broadcast_to(pad_lanes(best, width), (8, width))
    reach = peers // 2
    pitch = -(-block // LANES) * LANES
    cap = out.shape[2] - pitch
    z, y = me_ref[0] // 2, me_ref[0] % 2
    none = jnp.full((1, cap), -1.0, jnp.float32)
    for k in range(peers):
        piece = best if k == 0 else pltpu.roll(best, width - k * block, 1)
        up = (z % 2 == 0) == (k % 2 == 1)
        row = z + jnp.where(up, k % reach, reach - k % reach)
        row = 2 * (row % reach) + (y if k < reach else 1 - y)
        out[row, :, :pitch] = piece[0:1, :pitch]
        out[k, :, pitch:] = none
    lead = [lead_top[i : i + 1, :] for i in range(4)]
    out[2 * z + y, :, pitch:] = lead[0]
    out[2 * z + 1 - y, :, pitch:] = lead[1]
    if edges:
        for at, to in ((1, 0), (reach - 2, reach - 1)):

            @pl.when(z == at)
            def _():
                out[2 * to + y, :, pitch:] = lead[2]
                out[2 * to + 1 - y, :, pitch:] = lead[3]


def final_kernel(peers, cap, info_ref, back_ref, out):
    count = info_ref.shape[1]
    pitch = back_ref.shape[2] - cap
    where = info_ref[1:2, :]
    rows = [back_ref[h] for h in range(peers)]
    lead = functools.reduce(jnp.maximum, [row[:, pitch:] for row in rows])
    total = jnp.zeros((1, count), jnp.float32)
    at = lax.broadcasted_iota(jnp.int32, (pitch, count), 0)
    cols = jnp.transpose(jnp.concatenate([row[:, :pitch] for row in rows], axis=0))
    for h in range(peers):
        hit = at + h * pitch == where
        total += jnp.sum(jnp.where(hit, cols[:, h : h + 1], 0.0), axis=0, keepdims=True)
    at = lax.broadcasted_iota(jnp.int32, (cap, count), 0) + peers * pitch
    total += jnp.sum(jnp.where(at == where, as_column(lead), 0.0), axis=0, keepdims=True)
    out[...] = total


def call(kernel, name, outs, in_specs, out_specs, scratch=(), flops=0, nbytes=0):
    return pl.pallas_call(
        kernel,
        name=name,
        out_shape=outs,
        in_specs=in_specs,
        out_specs=out_specs,
        scratch_shapes=list(scratch),
        compiler_params=pltpu.CompilerParams(vmem_limit_bytes=VMEM_LIMIT),
        cost_estimate=pl.CostEstimate(flops=flops, bytes_accessed=nbytes, transcendentals=0),
    )


def whole_exchange(embeddings, cluster_ids):
    count, width = embeddings.shape
    peers = lax.axis_size("dp")
    slots = 2 * count // peers
    squares = jnp.sum(embeddings * embeddings, axis=1, keepdims=True)
    unit = (embeddings * lax.rsqrt(squares + 1e-06)).astype(jnp.bfloat16)
    target = cluster_ids // CL_DEV
    onehot = (target[:, None] == jnp.arange(peers, dtype=jnp.int32)[None, :]).astype(jnp.int32)
    ranking = jnp.cumsum(onehot, axis=0) - 1
    position = jnp.sum(ranking * onehot, axis=1)
    where_to = target * slots + position
    total = peers * slots
    send_rows = jnp.zeros((total, width), jnp.bfloat16).at[where_to].set(unit)
    send_ids = jnp.full((total,), -1, jnp.int32).at[where_to].set(cluster_ids)
    own_rows = lax.all_to_all(send_rows, "dp", split_axis=0, concat_axis=0, tiled=True)
    own_ids = lax.all_to_all(send_ids, "dp", split_axis=0, concat_axis=0, tiled=True)
    swap = [(0, 1), (1, 0)]
    far_rows = lax.ppermute(own_rows, "owner", swap)
    far_ids = lax.ppermute(own_ids, "owner", swap)
    block = math.gcd(total, 512)
    column_pos = jnp.arange(total, dtype=jnp.int32)

    def block_best(start):
        queries = lax.dynamic_slice_in_dim(own_rows, start, block, 0)
        query_ids = lax.dynamic_slice_in_dim(own_ids, start, block, 0)
        row_pos = start + jnp.arange(block, dtype=jnp.int32)
        tops = []
        for rows, ids, own in ((own_rows, own_ids, True), (far_rows, far_ids, False)):
            scores = lax.dot_general(queries, rows, NT, preferred_element_type=jnp.float32)
            same = (query_ids[:, None] == ids[None, :]) & (ids[None, :] >= 0)
            if own:
                same = same & (row_pos[:, None] != column_pos[None, :])
            tops.append(jnp.max(jnp.where(same, scores, jnp.float32(-1.0)), axis=1))
        return jnp.maximum(tops[0], tops[1])

    starts = jnp.arange(total // block, dtype=jnp.int32) * block
    best = lax.map(block_best, starts).reshape(peers, slots)
    returned = lax.all_to_all(best, "dp", split_axis=0, concat_axis=0, tiled=True)
    return returned.reshape(-1)[where_to]


def local(embeddings, cluster_ids):
    count, width = embeddings.shape
    peers = lax.axis_size("dp")
    groups = lax.axis_size("groups")
    cap = 2 * count // peers
    mean = -(-(count - cap) // (peers - 1))
    block = -(-(mean + 1) // SUB) * SUB
    slots = peers * block
    pitch = -(-block // LANES) * LANES
    reach = peers // 2
    bf16, f32 = jnp.bfloat16, jnp.float32
    shape = jax.ShapeDtypeStruct
    me = lax.axis_index("dp")
    me1 = me.reshape(1)

    def dp_pairs(step):
        pairs = []
        for z in range(reach):
            for y in range(2):
                to = step(z, y)
                if to is not None:
                    pairs.append((2 * z + y, 2 * to[0] + to[1]))
        return pairs

    other_y = dp_pairs(lambda z, y: (z, 1 - y))
    up_pairs = dp_pairs(lambda z, y: (z + 1, y) if z + 1 < reach else None)
    down_pairs = dp_pairs(lambda z, y: (z - 1, y) if z > 0 else None)
    swap = [(0, 1), (1, 0)]

    ends_pairs = dp_pairs(lambda z, y: (reach - 1 - z, y) if z in (0, reach - 1) else None)
    shift_pairs = [
        dp_pairs(lambda z, y, s=s: ((z + (s if z % 2 == 0 else reach - s)) % reach, y)) for s in range(2, reach - 1)
    ]
    even_pairs = dp_pairs(lambda z, y: (z ^ 1, y))
    odd_pairs = dp_pairs(lambda z, y: (((z + 1) ^ 1) - 1, y) if 0 < z < reach - 1 else None)

    one = shape((block, width), bf16)
    lead_rows = cap + SUB
    message = shape((lead_rows + block, width), bf16)
    edges = reach == 4

    info, mine, mine_across, even, odd, across, *fars = call(
        functools.partial(pack_kernel, peers, cap, block),
        "pack",
        [shape((8, count), jnp.int32), one, one, message, message]
        + [shape(((reach - 1) * block, width), bf16)]
        + [one] * (reach - 3),
        [SMEM, VMEM, pl.BlockSpec(memory_space=pltpu.HBM)],
        [VMEM] * (3 + reach),
        [
            pltpu.VMEM((count, width), f32),
            pltpu.VMEM((count, width), bf16),
            pltpu.VMEM((slots + cap, count), bf16),
            pltpu.SemaphoreType.DMA((CHUNKS,)),
        ],
        flops=2 * (slots + cap) * count * width,
        nbytes=8 * count * width,
    )(me1, cluster_ids.reshape(1, count), embeddings)
    odd1 = lax.ppermute(odd, "dp", odd_pairs)
    even1 = lax.ppermute(even, "dp", even_pairs)
    across = lax.ppermute(across, "dp", other_y)
    fars = [lax.ppermute(rows, "dp", pairs) for rows, pairs in zip(fars, shift_pairs)]
    across, even1, fars = lax.optimization_barrier((across, even1, fars))
    odd2, ends, asked, near_cols, *fars_r = call(
        functools.partial(relay_kernel, peers, block, lead_rows),
        "relay",
        [
            message,
            shape((2 * block, width), bf16),
            shape((2 * lead_rows + block, width), bf16),
            shape((2 * lead_rows, width), bf16),
        ]
        + [one] * (reach - 3),
        [VMEM] * 5,
        [VMEM] * (1 + reach),
        nbytes=2 * slots * width,
    )(even, odd, mine_across, across, even1)
    odd2 = lax.ppermute(odd2, "dp", odd_pairs)
    asked_y = lax.ppermute(asked, "dp", other_y)
    near_o = lax.ppermute(near_cols, "owner", swap)
    even2 = call(
        functools.partial(pass_kernel, block, lead_rows),
        "pass_on",
        message,
        [VMEM] * 2,
        VMEM,
        nbytes=8 * lead_rows * width,
    )(odd1, across)
    even2 = lax.ppermute(even2, "dp", even_pairs)
    ends = lax.ppermute(ends, "dp", ends_pairs)
    fars_r = [lax.ppermute(rows, "dp", pairs) for rows, pairs in zip(fars_r, shift_pairs)]
    odd2, asked_y, near_cols, near_o = lax.optimization_barrier((odd2, asked_y, near_cols, near_o))
    early = call(
        functools.partial(lead_early_kernel, cap),
        "lead_early",
        shape((8, cap), f32),
        [VMEM] * 4,
        VMEM,
        flops=24 * cap * cap * width,
        nbytes=14 * cap * width,
    )(asked, asked_y, near_cols, near_o)
    odd2, even2, ends, fars_r, asked_y, early = lax.optimization_barrier((odd2, even2, ends, fars_r, asked_y, early))
    late = []
    if not edges:
        is_even = (me // 2) % 2 == 0
        up = jnp.where(is_even, odd2[:lead_rows], even2[:lead_rows])
        down = jnp.where(is_even, even2[:lead_rows], odd2[:lead_rows])
        late = [up, down]
        for _ in range(reach - 3):
            up = lax.ppermute(up, "dp", up_pairs)
            down = lax.ppermute(down, "dp", down_pairs)
            late += [up, down]
    own, first, second = call(
        functools.partial(collect_kernel, peers, block, lead_rows),
        "collect",
        [
            shape((slots, width), bf16),
            shape((FIRST * block + (1 + max(1, len(late))) * lead_rows, width), bf16),
            shape((slots - FIRST * block, width), bf16),
        ],
        [SMEM] + [VMEM] * (7 + 2 * (reach - 3) + len(late)),
        [VMEM] * 3,
        nbytes=4 * slots * width,
    )(me1, mine, even1, odd1, asked_y, even2, odd2, ends, *fars, *fars_r, *late)
    first_o = lax.ppermute(first, "owner", swap)
    second_o = lax.ppermute(second, "owner", swap)
    lead_top = call(
        functools.partial(lead_best_kernel, cap, block),
        "lead_best",
        shape((8, cap), f32),
        [VMEM] * 4,
        VMEM,
        flops=40 * cap * cap * width,
        nbytes=20 * cap * width,
    )(early, asked, asked_y, first)
    top = call(
        functools.partial(own_best_kernel, peers, block),
        "own_best",
        shape((8, slots), f32),
        [VMEM],
        VMEM,
        flops=2 * slots * slots * width,
        nbytes=2 * slots * width,
    )(own)
    top, lead_top = call(
        functools.partial(first_best_kernel, peers, block, cap),
        "first_best",
        [shape((8, slots), f32), shape((8, cap), f32)],
        [VMEM] * 6,
        [VMEM] * 2,
        flops=2 * FIRST * block * slots * width + 14 * cap * cap * width,
        nbytes=4 * slots * width,
    )(own, first_o, top, asked, asked_y, lead_top)
    best, flag = call(
        functools.partial(far_best_kernel, peers, block, edges),
        "far_best",
        [shape((peers, 1, pitch + cap), f32), shape((8, LANES), f32)],
        [SMEM] + [VMEM] * 4,
        [VMEM] * 2,
        flops=2 * slots * slots * width,
        nbytes=4 * slots * width,
    )(me1, own, second_o, top, lead_top)
    back = lax.all_to_all(best, "dp", split_axis=0, concat_axis=0, tiled=True)
    flags = [flag]
    for k in range(1, groups):
        flags.append(lax.ppermute(flag, "groups", [(g, (g + k) % groups) for g in range(groups)]))
    odd = functools.reduce(jnp.maximum, flags)[0, 0]
    select = call(
        functools.partial(final_kernel, peers, cap),
        "final",
        shape((1, count), f32),
        [VMEM] * 2,
        VMEM,
        flops=0,
        nbytes=4 * count,
    )
    return lax.cond(odd > 0, whole_exchange, lambda e, c: select(info, back).reshape(count), embeddings, cluster_ids)


def solution(mesh):
    return jax.shard_map(
        local,
        mesh=mesh,
        in_specs=(P(("groups", "dp", "owner"), None), P(("groups", "dp", "owner"))),
        out_specs=P(("groups", "dp", "owner")),
        check_vma=False,
    )
```
